256 devices in a mesh: tm: 128 (over z, y, x), space: 2 (over core).
Axes of the slice: x: 4, y: 4, z: 8, core: 2. Of those that a mesh axis runs over, the one named last changes fastest.
Arguments:
- features: bfloat16 [256, 128, 2048], P('tm', 'space'), may hold values from -24 to 24
- queries: bfloat16 [256, 128, 1024], P('tm', 'space'), may hold values from -144 to 144
- cotangent: bfloat16 [256, 128, 1024], P('tm', 'space'), may hold values from -6 to 6
- key_weight: bfloat16 [2048, 1024], P(None, 'space'), may hold values from -0.125 to 0.125
- value_weight: bfloat16 [2048, 1024], P(None, 'space'), may hold values from -0.125 to 0.125
Outputs:
- attended: bfloat16 [256, 128, 1024], P('tm', 'space')
- grad_features: bfloat16 [256, 128, 2048], P('tm', 'space')
- grad_queries: bfloat16 [256, 128, 1024], P('tm', 'space')
- grad_key_weight: float32 [2048, 1024], P('tm', 'space')
- grad_value_weight: float32 [2048, 1024], P('tm', 'space')
The draws below stay inside these ranges and needn't reach their ends.
All inputs are finite; a program needn't handle non-finite values.
Results may differ from the reference program's by a relative error of at most 0.025.
The reference program's roundings to bfloat16 on the way (of `key_rows`, `value_rows`, `rounded`, `dscore`, `grad_keys` and `grad_values`) count: a program that leaves them out, or rounds other values in their place, can miss the bound.
Values may be sent and summed in bfloat16 or wider, within the bound.
A program may use at most 128 MiB of HBM per device.

```python
import jax
import jax.numpy as jnp
from jax import lax

D = 2048
HEADS = 8
HEAD = 128
PATCH = 128
WINDOW = 16
FR_DEV = 2
INNER = 1024
FRAMES = 256


def draw_queries(key, part):
    key = jax.random.fold_in(key, 7)
    normal_part = jax.random.normal(key, (FRAMES, PATCH, HEADS * HEAD), jnp.float32)
    return jnp.clip(normal_part, -6.0, 6.0).astype(jnp.bfloat16)


def raised(result, rng, source, target, parts, factor):
    owner, partner = [(jnp.arange(result.shape[position]) // (result.shape[position] // parts)).reshape([-1 if axis == position else 1 for axis in range(result.ndim)]) for position in (source, target)]
    chosen = jax.random.permutation(rng, parts)[partner]
    strong = (owner == chosen) | (owner == (partner + parts // 2) % parts)
    return jnp.where(strong, factor * result, result)


def level_of(own_key, extent, shards, least, high):
    def one(dim, parts):
        draws = jax.random.uniform(jax.random.fold_in(jax.random.fold_in(own_key, 6), dim), (parts,), jnp.float32, least / len(shards), high / len(shards))
        return jnp.repeat(jnp.exp(draws), extent[dim] // parts).reshape((-1,) + (1,) * (len(extent) - dim - 1))

    loudness = one(*shards[0])
    for cut in shards[1:]:
        loudness = loudness * one(*cut)
    return loudness


def centred(key, dims, scale, limit, pieces=(), kind=jnp.bfloat16):
    array = jax.random.normal(key, dims, jnp.float32) * scale
    if len(pieces) > 0:
        array = level_of(key, dims, pieces, -0.22, 0.18) * array
    return jnp.clip(array, min=-limit, max=limit).astype(kind)


def bell_draw_with(stream_key, shape, deviation, limit, pieces, heavy, kind=jnp.bfloat16):
    values = deviation * jax.random.normal(stream_key, shape, jnp.float32)
    if pieces:
        values = values * level_of(stream_key, shape, pieces, -0.22, 0.18)
    return jnp.clip(raised(values, jax.random.fold_in(stream_key, 3), *heavy), -limit, limit).astype(kind)


def setup_inputs(seed: int = 0) -> dict:
    keys = jax.random.split(jax.random.key(seed), 6)
    return {
        "features": bell_draw_with(keys[0], (FRAMES, PATCH, D), 1.0, 24.0, ((0, 128), (1, 2)), (0, 2, 128, 5.5)),
        "queries": draw_queries(jax.random.fold_in(keys[5], 71), 0),
        "cotangent": centred(keys[2], (FRAMES, PATCH, INNER), 1.0, 6.0, ((0, 128), (1, 2))),
        "key_weight": centred(keys[3], (D, INNER), D ** -0.5, 0.125, ((1, 2),)),
        "value_weight": centred(keys[4], (D, INNER), D ** -0.5, 0.125, ((1, 2),)),
    }


def window_allowed(query_pos, key_pos, reach_back, lowest):
    later = key_pos[None, :] <= query_pos[:, None]
    inside = key_pos[None, :] >= query_pos[:, None] - reach_back
    return later & inside & (key_pos[None, :] >= lowest)


def block_attend(queries_in, grad_out, key_rows, value_rows, allowed):
    scale = HEAD ** -0.5
    scores = jnp.einsum("tphe,uphe->phtu", queries_in.astype(jnp.float32), key_rows.astype(jnp.float32)) * scale
    scores = jnp.where(allowed, scores, -jnp.inf)
    row_top = jnp.max(scores, axis=-1, keepdims=True)
    row_total = jnp.log(jnp.sum(jnp.exp(scores - row_top), axis=-1, keepdims=True)) + row_top
    weights = jnp.exp(scores - row_total)
    rounded = weights.astype(jnp.bfloat16)
    dprobs = jnp.einsum("tphe,uphe->phtu", grad_out.astype(jnp.float32), value_rows.astype(jnp.float32))
    spread = jnp.sum(weights * dprobs, axis=-1, keepdims=True)
    dscore = (weights * (dprobs - spread) * scale).astype(jnp.bfloat16)
    attended = jnp.einsum("phtu,uphe->tphe", rounded.astype(jnp.float32), value_rows.astype(jnp.float32))
    grad_query = jnp.einsum("phtu,uphe->tphe", dscore.astype(jnp.float32), key_rows.astype(jnp.float32))
    grad_keys = jnp.einsum("phtu,tphe->uphe", dscore.astype(jnp.float32), queries_in.astype(jnp.float32))
    grad_values = jnp.einsum("phtu,tphe->uphe", rounded.astype(jnp.float32), grad_out.astype(jnp.float32))
    return attended.astype(jnp.bfloat16), grad_query.astype(jnp.bfloat16), grad_keys, grad_values


def reference(features, queries, cotangent, key_weight, value_weight):
    reach_back = WINDOW - 1
    flat_rows = features.reshape(FRAMES * PATCH, D)
    key_all = jnp.dot(flat_rows, key_weight, preferred_element_type=jnp.float32).astype(jnp.bfloat16).reshape(FRAMES, PATCH, INNER)
    value_all = jnp.dot(flat_rows, value_weight, preferred_element_type=jnp.float32).astype(jnp.bfloat16).reshape(FRAMES, PATCH, INNER)
    leading = jnp.zeros((reach_back, PATCH, INNER), jnp.bfloat16)
    key_padded = jnp.concatenate([leading, key_all], axis=0)
    value_padded = jnp.concatenate([leading, value_all], axis=0)
    span_rows = FR_DEV + reach_back
    query_pos = jnp.arange(FR_DEV, dtype=jnp.int32) + reach_back
    key_pos = jnp.arange(span_rows, dtype=jnp.int32)

    def block_step(carry, block_index):
        key_acc, value_acc = carry
        first_frame = (block_index * FR_DEV).astype(jnp.int32)
        key_block = lax.dynamic_slice_in_dim(key_padded, first_frame, span_rows, 0).reshape(span_rows, PATCH, HEADS, HEAD)
        value_block = lax.dynamic_slice_in_dim(value_padded, first_frame, span_rows, 0).reshape(span_rows, PATCH, HEADS, HEAD)
        query_block = lax.dynamic_slice_in_dim(queries, first_frame, FR_DEV, 0).reshape(FR_DEV, PATCH, HEADS, HEAD)
        cot_block = lax.dynamic_slice_in_dim(cotangent, first_frame, FR_DEV, 0).reshape(FR_DEV, PATCH, HEADS, HEAD)
        allowed = window_allowed(query_pos, key_pos, reach_back, reach_back - first_frame)
        attended, grad_query, grad_keys, grad_values = block_attend(query_block, cot_block, key_block, value_block, allowed)
        key_acc = key_acc + grad_keys.reshape(span_rows, PATCH, INNER)
        value_acc = value_acc + grad_values.reshape(span_rows, PATCH, INNER)
        key_done = key_acc[:FR_DEV].astype(jnp.bfloat16)
        value_done = value_acc[:FR_DEV].astype(jnp.bfloat16)
        trailing = jnp.zeros((FR_DEV, PATCH, INNER), jnp.float32)
        key_acc = jnp.concatenate([key_acc[FR_DEV:], trailing], axis=0)
        value_acc = jnp.concatenate([value_acc[FR_DEV:], trailing], axis=0)
        return (key_acc, value_acc), (attended.reshape(FR_DEV, PATCH, INNER), grad_query.reshape(FR_DEV, PATCH, INNER), key_done, value_done)

    start_acc = jnp.zeros((span_rows, PATCH, INNER), jnp.float32)
    blocks = FRAMES // FR_DEV
    final_carry, stacked = lax.scan(block_step, (start_acc, start_acc), jnp.arange(blocks, dtype=jnp.int32))
    attended = stacked[0].reshape(FRAMES, PATCH, INNER)
    grad_queries = stacked[1].reshape(FRAMES, PATCH, INNER)
    grad_keys = jnp.concatenate([stacked[2].reshape(FRAMES, PATCH, INNER)[reach_back:], final_carry[0][:reach_back].astype(jnp.bfloat16)], axis=0)
    grad_values = jnp.concatenate([stacked[3].reshape(FRAMES, PATCH, INNER)[reach_back:], final_carry[1][:reach_back].astype(jnp.bfloat16)], axis=0)
    key_flat = grad_keys.reshape(FRAMES * PATCH, INNER)
    value_flat = grad_values.reshape(FRAMES * PATCH, INNER)
    grad_features = jnp.dot(key_flat, key_weight.T, preferred_element_type=jnp.float32) + jnp.dot(value_flat, value_weight.T, preferred_element_type=jnp.float32)
    grad_features = grad_features.astype(jnp.bfloat16).reshape(FRAMES, PATCH, D)
    grad_key_weight = jnp.dot(flat_rows.T, key_flat, preferred_element_type=jnp.float32)
    grad_value_weight = jnp.dot(flat_rows.T, value_flat, preferred_element_type=jnp.float32)
    return attended, grad_features, grad_queries, grad_key_weight, grad_value_weight
```

```python
import jax
import jax.numpy as jnp
from jax import lax
from jax.experimental import pallas as pl
from jax.experimental.pallas import tpu as pltpu
from jax.sharding import PartitionSpec as P

HEAD = 128
WINDOW = 16
PLANE = 16
NZ = 8
OWN = 256
HALO = 128
F32 = jnp.float32
BF16 = jnp.bfloat16
VM = pltpu.VMEM
MIB = 2**20


def mm(a, b, ca, cb):
    return lax.dot_general(a, b, (((ca,), (cb,)), ((), ())), preferred_element_type=F32)


def place():
    tm = lax.axis_index("tm")
    return tm // PLANE, tm % PLANE, lax.axis_index("space")


def remote(src, dst, ssem, rsem, tm, core):
    return pltpu.make_async_remote_copy(
        src_ref=src, dst_ref=dst, send_sem=ssem, recv_sem=rsem,
        device_id=(tm, core), device_id_type=pl.DeviceIdType.MESH,
    )


def rows_at(ref, start, count):
    return ref.at[pl.ds(pl.multiple_of(start, 16), count)]


def signal(sem, tm, core):
    pl.semaphore_signal(
        sem, inc=1, device_id=(tm, core), device_id_type=pl.DeviceIdType.MESH
    )


def await_bytes(ref, sem):
    pltpu.make_async_copy(ref, ref, sem).wait()


class Sends:
    def __init__(self, sems):
        self.sems, self.used, self.waits = sems, 0, []

    def start(self, src, dst, rsem, tm, core, self_if=None):
        copy = remote(src, dst, self.sems.at[self.used], rsem, tm, core)
        self.used += 1
        if self_if is None:
            copy.start()
        else:
            pl.when(self_if)(lambda: pltpu.make_async_copy(src, dst, rsem).start())
            pl.when(jnp.logical_not(self_if))(copy.start)
        self.waits.append((copy, self_if))

    def finish(self):
        for copy, self_if in self.waits:
            if self_if is None:
                copy.wait_send()
            else:
                pl.when(jnp.logical_not(self_if))(copy.wait_send)


def exchange_kernel(f_ref, qc_ref, rows_ref, qco_ref, send, got):
    z, c, s = place()
    base = z * PLANE
    nxt = ((z + 1) % NZ) * PLANE + c
    prv = ((z + NZ - 1) % NZ) * PLANE + c
    mine = c % 2 == s
    barrier = pltpu.get_barrier_semaphore()
    for r in range(1, PLANE):
        signal(barrier, base + (c + r) % PLANE, c % 2)
    signal(barrier, base + c, 1 - s)
    signal(barrier, prv, s)
    pl.semaphore_wait(barrier, jnp.where(mine, 16, 18))

    sends = Sends(send)
    to = (c // 4) % 2
    for r in range(8):
        j = (c // 2 + r) % 8
        d = 2 * j + s
        sends.start(
            rows_at(f_ref, 16 * j, 16), rows_at(rows_ref, HALO + 16 * c, 16),
            got.at[c // 8], base + d, to, (mine & (to == s)) if r == 0 else None,
        )
    for r in range(8):
        j = (c // 2 + r) % 8
        d = 2 * j + s
        for o in range(2):
            core = (s + o) % 2
            sends.start(
                rows_at(qc_ref.at[core], 16 * j, 16), rows_at(qco_ref, 16 * c, 16),
                got.at[2], base + d, core, mine if r == 0 and o == 0 else None,
            )
    late = rows_at(rows_ref, HALO + 128 + 64 * s, 64)
    await_bytes(late, got.at[1])
    halo_there = rows_at(rows_ref, 64 * s, 64)
    sends.start(late, halo_there, got.at[3], nxt, s)
    sends.start(late, late, got.at[5], base + c, 1 - s)
    early = rows_at(rows_ref, HALO + 64 * s, 64)
    await_bytes(early, got.at[0])
    sends.start(early, early, got.at[4], base + c, 1 - s)
    await_bytes(halo_there, got.at[3])
    sends.start(halo_there, halo_there, got.at[6], base + c, 1 - s)
    await_bytes(qco_ref, got.at[2])
    await_bytes(rows_at(rows_ref, HALO + 64 * (1 - s), 64), got.at[4])
    await_bytes(rows_at(rows_ref, HALO + 128 + 64 * (1 - s), 64), got.at[5])
    await_bytes(rows_at(rows_ref, 64 * (1 - s), 64), got.at[6])
    sends.finish()


def exchange(f, qc):
    d, width = f.shape[1], qc.shape[2]
    return pl.pallas_call(
        exchange_kernel,
        out_shape=(
            jax.ShapeDtypeStruct((HALO + OWN, d), BF16),
            jax.ShapeDtypeStruct((OWN, width), BF16),
        ),
        in_specs=[pl.BlockSpec(memory_space=VM)] * 2,
        out_specs=[pl.BlockSpec(memory_space=VM)] * 2,
        scratch_shapes=[pltpu.SemaphoreType.DMA((28,)), pltpu.SemaphoreType.DMA((7,))],
        compiler_params=pltpu.CompilerParams(
            collective_id=0, has_side_effects=True, vmem_limit_bytes=16 * MIB
        ),
    )(f, qc)


def local_kernel(
    rows_ref, qc_ref, kw_ref, vw_ref, ag_ref, gf_ref, wa_ref, wb_ref, wc_ref,
    k_scr, v_scr, g_scr, acc_scr
):
    z, _, _ = place()
    half = kw_ref.shape[1]
    scale = HEAD ** -0.5
    n = OWN // 2
    k_scr[...] = mm(rows_ref[...], kw_ref[...], 1, 0).astype(BF16)
    v_scr[...] = mm(rows_ref[...], vw_ref[...], 1, 0).astype(BF16)
    acc_scr[...] = jnp.zeros_like(acc_scr)
    back = (
        lax.broadcasted_iota(jnp.int32, (n, 2 * n), 0) + HALO
        - lax.broadcasted_iota(jnp.int32, (n, 2 * n), 1)
    )
    window = (back >= 0) & (back < 8 * WINDOW) & (back % 8 == 0)
    halo_key = lax.broadcasted_iota(jnp.int32, (n, 2 * n), 1) < HALO
    for tile in range(2):
        lo = tile * n
        allowed = window & ((z > 0) | jnp.logical_not(halo_key)) if tile == 0 else window
        for h in range(half // HEAD):
            cols = slice(h * HEAD, (h + 1) * HEAD)
            vcols = slice(half + h * HEAD, half + (h + 1) * HEAD)
            q = qc_ref[lo : lo + n, cols]
            c = qc_ref[lo : lo + n, vcols]
            k = k_scr[lo : lo + 2 * n, cols]
            v = v_scr[lo : lo + 2 * n, cols]
            scores = jnp.where(allowed, mm(q, k, 1, 1) * scale, -jnp.inf)
            top = jnp.max(scores, axis=-1, keepdims=True)
            total = jnp.log(jnp.sum(jnp.exp(scores - top), axis=-1, keepdims=True)) + top
            w = jnp.exp(scores - total)
            rounded = w.astype(BF16)
            dp = mm(c, v, 1, 1)
            spread = jnp.sum(w * dp, axis=-1, keepdims=True)
            ds = (w * (dp - spread) * scale).astype(BF16)
            ag_ref[lo : lo + n, cols] = mm(rounded, v, 1, 0).astype(BF16)
            ag_ref[lo : lo + n, vcols] = mm(ds, k, 1, 0).astype(BF16)
            acc_scr[lo : lo + 2 * n, cols] += mm(ds, q, 0, 0)
            acc_scr[lo : lo + 2 * n, vcols] += mm(rounded, c, 0, 0)
    g_scr[...] = acc_scr[...].astype(BF16)
    at = 0
    for ref in (wa_ref, wb_ref, wc_ref):
        w = ref.shape[1]
        ref[...] = mm(rows_ref[...], g_scr[:, at : at + w], 0, 0).astype(BF16)
        at += w
    gf = mm(g_scr[:, :half], kw_ref[...], 1, 1) + mm(g_scr[:, half:], vw_ref[...], 1, 1)
    gf_ref[...] = gf.astype(BF16)


PARTS = (384, 384, 256)


def local(rows, qc, kw, vw):
    n_all, d = rows.shape
    n_own, width = qc.shape
    half = width // 2
    return pl.pallas_call(
        local_kernel,
        out_shape=(
            jax.ShapeDtypeStruct((n_own, width), BF16),
            jax.ShapeDtypeStruct((n_all, d), BF16),
        ) + tuple(jax.ShapeDtypeStruct((d, w), BF16) for w in PARTS),
        in_specs=[pl.BlockSpec(memory_space=VM)] * 4,
        out_specs=[pl.BlockSpec(memory_space=VM)] * 5,
        scratch_shapes=[
            pltpu.VMEM((n_all, half), BF16),
            pltpu.VMEM((n_all, half), BF16),
            pltpu.VMEM((n_all, width), BF16),
            pltpu.VMEM((n_all, width), F32),
        ],
        compiler_params=pltpu.CompilerParams(vmem_limit_bytes=48 * MIB),
    )(rows, qc, kw, vw)


class Ring4:
    def __init__(self, sends, view, up, down, bufs, sems, out):
        self.sends, self.view, self.up, self.down = sends, view, up, down
        self.bufs, self.sems, self.out = bufs, sems, out

    def first(self):
        from_below, from_above, below, above = self.bufs
        h = below.shape[0] // 2
        self.sends.start(self.view(2, 0), from_below, self.sems.at[0], *self.up)
        self.sends.start(self.view(2, 1), from_above, self.sems.at[1], *self.down)
        self.sends.start(self.view(1, 1), below.at[pl.ds(h, h)], self.sems.at[2], *self.up)
        self.sends.start(self.view(3, 0), above.at[pl.ds(0, h)], self.sems.at[3], *self.down)

    def second(self):
        from_below, from_above, below, above = self.bufs
        h = below.shape[0] // 2
        for buf, sem, view, dst, dsem, dev in (
            (from_below, 0, self.view(1, 0), below.at[pl.ds(0, h)], 4, self.up),
            (from_above, 1, self.view(3, 1), above.at[pl.ds(h, h)], 5, self.down),
        ):
            await_bytes(buf, self.sems.at[sem])

            def add(i, _):
                buf[i] = (buf[i].astype(F32) + view[i].astype(F32)).astype(BF16)
                return 0

            lax.fori_loop(0, h, add, 0)
            self.sends.start(buf, dst, self.sems.at[dsem], *dev)

    def third(self):
        from_below, from_above, below, above = self.bufs
        h = below.shape[0] // 2
        await_bytes(below.at[pl.ds(h, h)], self.sems.at[2])
        await_bytes(above.at[pl.ds(0, h)], self.sems.at[3])
        await_bytes(below.at[pl.ds(0, h)], self.sems.at[4])
        await_bytes(above.at[pl.ds(h, h)], self.sems.at[5])
        for half in range(2):
            own = self.view(0, half)

            def add(i, _):
                j = half * h + i
                self.out[j] = (
                    own[i].astype(F32) + below[j].astype(F32) + above[j].astype(F32)
                ).astype(BF16)
                return 0

            lax.fori_loop(0, h, add, 0)


def return_kernel(
    ag_ref, gf_ref, wa_ref, wb_ref, wc_ref, rag_ref, rgf_ref, gk_ref, gv_ref,
    gx, gh, a1, a2, a3, a4, ra, a5, a6, a7, a8, ra2, za,
    b1, b2, b3, b4, rb, b5, b6, b7, b8, rb2, zb, cb, rc, cc,
    send, gsem, a1sem, a2sem, b1sem, b2sem, csem, fsem
):
    z, c, s = place()
    y, x = c // 4, c % 4
    base = z * PLANE
    prv = ((z + NZ - 1) % NZ) * PLANE + c
    nxt = ((z + 1) % NZ) * PLANE + c
    barrier = pltpu.get_barrier_semaphore()
    for r in range(1, PLANE):
        for core in range(2):
            signal(barrier, base + (c + r) % PLANE, core)
    signal(barrier, base + c, 1 - s)
    for r in range(1, NZ):
        signal(barrier, ((z + r) % NZ) * PLANE + c, s)
    pl.semaphore_wait(barrier, 2 * (PLANE - 1) + 1 + NZ - 1)

    sends = Sends(send)
    home = c % 2
    slot = 16 * (c // 2)
    for r in range(PLANE):
        d = (c + r) % PLANE
        sends.start(
            rows_at(ag_ref, 16 * d, 16), rows_at(rag_ref.at[s], slot, 16),
            gsem.at[0], base + d, home, (home == s) if r == 0 else None,
        )
    for i in range(3):
        sends.start(
            rows_at(gf_ref, 128 * i + 64 * (1 - s), 64), gx.at[pl.ds(64 * i, 64)],
            gsem.at[1 + i], base + c, 1 - s,
        )

    def tm_x(v):
        return base + y * 4 + v

    def tm_y(v):
        return base + v * 4 + x

    xi = [(x + r) % 4 for r in range(4)]
    yi = [(y + r) % 4 for r in range(4)]
    zi = [(z + r) % NZ for r in range(NZ)]
    ring_a1 = Ring4(
        sends, lambda r, h: wa_ref.at[pl.ds(4 * h, 4), :, xi[r]],
        (tm_x(xi[1]), s), (tm_x(xi[3]), s), (a1, a2, a3, a4), a1sem, ra,
    )
    ring_b1 = Ring4(
        sends, lambda r, h: wb_ref.at[pl.ds(4 * h, 4), yi[r]],
        (tm_y(yi[1]), s), (tm_y(yi[3]), s), (b1, b2, b3, b4), b1sem, rb,
    )
    ring_a2 = Ring4(
        sends, lambda r, h: ra.at[pl.ds(4 * h, 4), yi[r]],
        (tm_y(yi[1]), s), (tm_y(yi[3]), s), (a5, a6, a7, a8), a2sem, ra2,
    )
    ring_b2 = Ring4(
        sends, lambda r, h: rb.at[pl.ds(4 * h, 4), xi[r]],
        (tm_x(xi[1]), s), (tm_x(xi[3]), s), (b5, b6, b7, b8), b2sem, rb2,
    )
    chains = ((1, 0, 4, 0), (-1, 1, 4, 4), (1, 1, 3, 8), (-1, 0, 3, 11))

    def c_view(rel, h):
        return wc_ref.at[zi[rel % NZ], pl.ds(2 * h, 2)]

    def c_step(k):
        for way, h, length, first in chains:
            if k >= length:
                continue
            dev = (nxt if way == 1 else prv, s)
            own = c_view(way * (length - k), h)
            if k == 0:
                src = own
            else:
                src = cb.at[first + k - 1]
                await_bytes(src, csem.at[first + k - 1])

                def add(i, _):
                    src[i] = (src[i].astype(F32) + own[i].astype(F32)).astype(BF16)
                    return 0

                lax.fori_loop(0, 2, add, 0)
            sends.start(src, cb.at[first + k], csem.at[first + k], *dev)

    ring_a1.first()
    ring_b1.first()
    c_step(0)

    def add_gf(i):
        await_bytes(gx.at[pl.ds(64 * i, 64)], gsem.at[1 + i])

        def add(t, _):
            there = pl.ds(pl.multiple_of(64 * i + 16 * t, 16), 16)
            here = pl.ds(pl.multiple_of(128 * i + 64 * s + 16 * t, 16), 16)
            gx[there] = (gx[there].astype(F32) + gf_ref[here].astype(F32)).astype(BF16)
            return 0

        lax.fori_loop(0, 4, add, 0)

    def gf_home(i):
        for r in range(4):
            t = (c + r) % 4
            d = 8 * (i - 1) + 4 * s + t
            sends.start(
                rows_at(gx, 64 * i + 16 * t, 16), rows_at(rgf_ref, slot, 16),
                gsem.at[5], base + d, home, ((d == c) & (home == s)) if r == 0 else None,
            )

    add_gf(0)
    sends.start(gx.at[pl.ds(0, 64)], gh, gsem.at[4], prv, s)
    add_gf(1)
    gf_home(1)
    add_gf(2)
    c_step(1)
    await_bytes(gh, gsem.at[4])

    def add_halo(t, _):
        there = pl.ds(pl.multiple_of(128 + 16 * t, 16), 16)
        here = pl.ds(pl.multiple_of(16 * t, 16), 16)
        gx[there] = (gx[there].astype(F32) + gh[here].astype(F32)).astype(BF16)
        return 0

    lax.fori_loop(0, 4, add_halo, 0)
    gf_home(2)
    ring_a1.second()
    ring_b1.second()
    c_step(2)
    ring_a1.third()
    ring_a2.first()
    ring_b1.third()
    ring_b2.first()
    c_step(3)
    ring_a2.second()
    ring_b2.second()
    for way, h, length, first in chains:
        await_bytes(cb.at[first + length - 1], csem.at[first + length - 1])
    for h, (p, m) in enumerate(((0, 3), (2, 1))):
        fp, fm = (chains[t][3] + chains[t][2] - 1 for t in (p, m))
        own = c_view(0, h)

        def add(i, _):
            rc[2 * h + i] = (
                own[i].astype(F32) + cb[fp, i].astype(F32) + cb[fm, i].astype(F32)
            ).astype(BF16)
            return 0

        lax.fori_loop(0, 2, add, 0)
    for r in range(1, PLANE):
        yy, xx = yi[r // 4], xi[r % 4]
        sends.start(rc.at[yy, xx], cc.at[r - 1], fsem.at[0], base + yy * 4 + xx, s)
    for ring, out, buf, sem in ((ring_a2, ra2, za, fsem.at[1]), (ring_b2, rb2, zb, fsem.at[2])):
        ring.third()
        for r in range(1, NZ):
            sends.start(out.at[zi[r]], buf.at[r - 1], sem, zi[r] * PLANE + c, s)

    def total(own, buf, count):
        return lax.fori_loop(
            0, count, lambda i, acc: acc + buf[i].astype(F32), own.astype(F32)
        )

    await_bytes(cc, fsem.at[0])
    gv_ref[:, 256:512] = total(rc[y, x], cc, PLANE - 1)
    await_bytes(za, fsem.at[1])
    gk_ref[:, 0:384] = total(ra2[z], za, NZ - 1)
    await_bytes(zb, fsem.at[2])
    last = total(rb2[z], zb, NZ - 1)
    gk_ref[:, 384:512] = last[:, :128]
    gv_ref[:, 0:256] = last[:, 128:]
    await_bytes(rag_ref, gsem.at[0])
    await_bytes(rgf_ref, gsem.at[5])
    sends.finish()


def give_back(ag, gf, wa, wb, wc):
    d = gf.shape[1]
    width = ag.shape[1]
    a, b, cw = PARTS

    def ring(w, mid):
        lead = (4, 4) if mid else (4,)
        full = (8, 4) if mid else (8,)
        return [pltpu.VMEM(lead + (16, w), BF16)] * 2 + [pltpu.VMEM(full + (16, w), BF16)] * 3

    sem = pltpu.SemaphoreType.DMA
    return pl.pallas_call(
        return_kernel,
        out_shape=(
            jax.ShapeDtypeStruct((2, 128, width), BF16),
            jax.ShapeDtypeStruct((128, d), BF16),
            jax.ShapeDtypeStruct((16, width // 2), F32),
            jax.ShapeDtypeStruct((16, width // 2), F32),
        ),
        in_specs=[pl.BlockSpec(memory_space=VM)] * 5,
        out_specs=[pl.BlockSpec(memory_space=VM)] * 4,
        scratch_shapes=[pltpu.VMEM((192, d), BF16), pltpu.VMEM((64, d), BF16)]
        + ring(a, True) + ring(a, False) + [pltpu.VMEM((7, 16, a), BF16)]
        + ring(b, True) + ring(b, False) + [pltpu.VMEM((7, 16, b), BF16)]
        + [
            pltpu.VMEM((14, 2, 4, 16, cw), BF16),
            pltpu.VMEM((4, 4, 16, cw), BF16),
            pltpu.VMEM((15, 16, cw), BF16),
            sem((128,)), sem((6,)), sem((6,)), sem((6,)), sem((6,)), sem((6,)), sem((14,)),
            sem((3,)),
        ],
        compiler_params=pltpu.CompilerParams(
            collective_id=1, has_side_effects=True, vmem_limit_bytes=48 * MIB
        ),
    )(ag, gf, *(w.reshape(8, 4, 4, 16, w.shape[1]) for w in (wa, wb, wc)))


def shards(features, queries, cotangent, key_weight, value_weight):
    frames, patches, d = features.shape
    half = key_weight.shape[1]

    def split(v):
        w = v.shape[2]
        return v.reshape(frames, 8, 8, w).transpose(1, 0, 2, 3).reshape(128, w)

    def join(v):
        w = v.shape[1]
        return v.reshape(8, frames, 8, w).transpose(1, 0, 2, 3).reshape(frames, patches, w)

    f, q, c = split(features), split(queries), split(cotangent)
    qc = jnp.stack(
        [jnp.concatenate([q[:, at : at + half], c[:, at : at + half]], axis=1) for at in (0, half)]
    )
    rows, qc = exchange(f, qc)
    ag, gf, wa, wb, wc = local(rows, qc, key_weight, value_weight)
    ag, gf, gk, gv = give_back(ag, gf, wa, wb, wc)
    att = join(jnp.concatenate([ag[0, :, :half], ag[1, :, :half]], axis=1))
    gq = join(jnp.concatenate([ag[0, :, half:], ag[1, :, half:]], axis=1))
    return att, join(gf), gq, gk, gv


def solution(mesh):
    rows = P("tm", "space", None)
    return jax.shard_map(
        shards,
        mesh=mesh,
        in_specs=(rows, rows, rows, P(None, "space"), P(None, "space")),
        out_specs=(rows, rows, rows, P("tm", "space"), P("tm", "space")),
        check_vma=False,
    )
```

```python
import jax
import jax.numpy as jnp
from jax import lax
from jax.experimental import pallas as pl
from jax.experimental.pallas import tpu as pltpu
from jax.sharding import PartitionSpec as P

HEAD = 128
WINDOW = 16
PLANE = 16
NZ = 8
OWN = 256
HALO = 128
ALL = HALO + OWN
HALF = 512
D = 2048
F32 = jnp.float32
BF16 = jnp.bfloat16
MIB = 2**20


def mm(a, b, ca, cb):
    return lax.dot_general(a, b, (((ca,), (cb,)), ((), ())), preferred_element_type=F32)


def rows_at(ref, start, count):
    return ref.at[pl.ds(pl.multiple_of(start, 16), count)]


def signal(sem, tm, core):
    pl.semaphore_signal(
        sem, inc=1, device_id=(tm, core), device_id_type=pl.DeviceIdType.MESH
    )


def await_bytes(ref, sem):
    pltpu.make_async_copy(ref, ref, sem).wait()


class Sends:
    def __init__(self, sems):
        self.sems, self.used, self.waits = sems, 0, []

    def start(self, src, dst, rsem, tm, core, self_if=None):
        copy = pltpu.make_async_remote_copy(
            src_ref=src, dst_ref=dst, send_sem=self.sems.at[self.used], recv_sem=rsem,
            device_id=(tm, core), device_id_type=pl.DeviceIdType.MESH,
        )
        self.used += 1
        if self_if is None:
            copy.start()
        else:
            pl.when(self_if)(lambda: pltpu.make_async_copy(src, dst, rsem).start())
            pl.when(jnp.logical_not(self_if))(copy.start)
        self.waits.append((copy, self_if))

    def finish(self):
        for copy, self_if in self.waits:
            if self_if is None:
                copy.wait_send()
            else:
                pl.when(jnp.logical_not(self_if))(copy.wait_send)


class Ring4:
    def __init__(self, sends, view, up, down, bufs, sems, out):
        self.sends, self.view, self.up, self.down = sends, view, up, down
        self.bufs, self.sems, self.out = bufs, sems, out

    def first(self):
        self.sends.start(self.view(2, 0), self.bufs[0], self.sems.at[0], *self.up)
        self.sends.start(self.view(2, 1), self.bufs[1], self.sems.at[1], *self.down)

    def direct(self):
        _, _, below, above = self.bufs
        h = below.shape[0] // 2
        self.sends.start(self.view(1, 1), below.at[pl.ds(h, h)], self.sems.at[2], *self.up)
        self.sends.start(self.view(3, 0), above.at[pl.ds(0, h)], self.sems.at[3], *self.down)

    def second(self):
        from_below, from_above, below, above = self.bufs
        h = below.shape[0] // 2
        for buf, sem, view, dst, dsem, dev in (
            (from_below, 0, self.view(1, 0), below.at[pl.ds(0, h)], 4, self.up),
            (from_above, 1, self.view(3, 1), above.at[pl.ds(h, h)], 5, self.down),
        ):
            await_bytes(buf, self.sems.at[sem])

            def add(i, _):
                buf[i] = (buf[i].astype(F32) + view[i].astype(F32)).astype(BF16)
                return 0

            lax.fori_loop(0, h, add, 0)
            self.sends.start(buf, dst, self.sems.at[dsem], *dev)

    def third(self):
        _, _, below, above = self.bufs
        h = below.shape[0] // 2
        await_bytes(below.at[pl.ds(h, h)], self.sems.at[2])
        await_bytes(above.at[pl.ds(0, h)], self.sems.at[3])
        await_bytes(below.at[pl.ds(0, h)], self.sems.at[4])
        await_bytes(above.at[pl.ds(h, h)], self.sems.at[5])
        for half in range(2):
            own = self.view(0, half)

            def add(i, _):
                j = half * h + i
                self.out[j] = (
                    own[i].astype(F32) + below[j].astype(F32) + above[j].astype(F32)
                ).astype(BF16)
                return 0

            lax.fori_loop(0, h, add, 0)


NQ = 2
CHAINS = ((1, 0, 4, 0), (-1, 1, 4, 4), (1, 1, 3, 8), (-1, 0, 3, 11))


def kernel(
    f_ref, q_ref, c_ref, kw_hbm, vw_hbm,
    att_out, gf_out, gq_out, gk_out, gv_out,
    kw, vw, fb, qcb, rows, qc, rt, k_scr, v_scr, acc, g, ag, gfp, rag, rgf, gx, gh,
    wa, wb, wc, ring_up, ring_down, ring_below, ring_above, plane_out,
    ring2_up, ring2_down, ring2_below, ring2_above, z_out, z_in, cb, rc, cc,
    send, wsem, got, fsem, hsem, gsem, r1sem, r2sem, csem, endsem,
):
    tm = lax.axis_index("tm")
    s = lax.axis_index("space")
    z, c = tm // PLANE, tm % PLANE
    y, x = c // 4, c % 4
    base = z * PLANE
    zi = [(z + r) % NZ for r in range(NZ)]
    yi = [(y + r) % 4 for r in range(4)]
    xi = [(x + r) % 4 for r in range(4)]
    nxt, prv = zi[1] * PLANE + c, zi[7] * PLANE + c

    weights = [
        pltpu.make_async_copy(kw_hbm, kw, wsem.at[0]),
        pltpu.make_async_copy(vw_hbm, vw, wsem.at[1]),
    ]
    for copy in weights:
        copy.start()
    barrier = pltpu.get_barrier_semaphore()
    for r in range(1, PLANE):
        for core in range(2):
            signal(barrier, base + (c + r) % PLANE, core)
    signal(barrier, base + c, 1 - s)
    for r in range(1, NZ):
        signal(barrier, zi[r] * PLANE + c, s)

    def pack(ref, out, cols, at):
        w = cols[1] - cols[0]
        for t in range(4):
            p, q = (ref[i, 16 * t : 16 * t + 16, cols[0] : cols[1]].astype(F32) for i in range(2))
            out[32 * t : 32 * t + 32, at : at + w] = jnp.concatenate(
                [p[:8], q[:8], p[8:], q[8:]], axis=0
            ).astype(BF16)

    pack(f_ref, fb, (0, D), 0)
    pl.semaphore_wait(barrier, 2 * (PLANE - 1) + 1 + NZ - 1)

    sends = Sends(send)
    to = (c // 4) % 2
    mine = c % 2 == s
    for r in range(8):
        j = (c // 2 + r) % 8
        sends.start(
            rows_at(fb, 16 * j, 16), rows_at(rows, HALO + 16 * c, 16), fsem.at[c],
            base + 2 * j + s, to, (mine & (to == s)) if r == 0 else None,
        )
    for core in range(2):
        pack(q_ref, qcb.at[core], (HALF * core, HALF * core + HALF), 0)
        pack(c_ref, qcb.at[core], (HALF * core, HALF * core + HALF), HALF)
    for r in range(4):
        i = 4 * s + xi[r]
        block = rows_at(rows, HALO + 128 + 16 * i, 16)
        await_bytes(block, fsem.at[8 + i])
        sends.start(block, rows_at(rows, 16 * i, 16), hsem.at[i], nxt, s)
        sends.start(block, block, got.at[0], base + c, 1 - s)
    for r in range(8):
        j = (c // 2 + r) % 8
        for o in range(2):
            core = (s + o) % 2
            sends.start(
                rows_at(qcb.at[core], 16 * j, 16), rows_at(qc, 16 * c, 16), got.at[3],
                base + 2 * j + s, core, mine if r == 0 and o == 0 else None,
            )
    for r in range(4):
        i = 4 * s + xi[r]
        block = rows_at(rows, HALO + 16 * i, 16)
        await_bytes(block, fsem.at[i])
        sends.start(block, block, got.at[1], base + c, 1 - s)

    def project(lo):
        part = rows[lo : lo + 128, :]
        k_scr[lo : lo + 128, :] = mm(part, kw[...], 1, 0).astype(BF16)
        v_scr[lo : lo + 128, :] = mm(part, vw[...], 1, 0).astype(BF16)
        rt[:, :, :, :, lo : lo + 128] = part.T.reshape(8, 4, 4, 16, 128)

    def other(lo):
        return rows_at(rows, lo + 64 * (1 - s), 64)

    for copy in weights:
        copy.wait()
    await_bytes(other(HALO + 128), got.at[0])
    project(HALO + 128)
    for r in range(4):
        i = 4 * s + xi[r]
        block = rows_at(rows, 16 * i, 16)
        await_bytes(block, hsem.at[i])
        sends.start(block, block, got.at[2], base + c, 1 - s)
    await_bytes(other(HALO), got.at[1])
    project(HALO)
    await_bytes(other(0), got.at[2])
    project(0)
    acc[...] = jnp.zeros_like(acc)
    await_bytes(qc, got.at[3])

    scale = HEAD ** -0.5
    n = OWN // 2
    col = lax.broadcasted_iota(jnp.int32, (n, 2 * n), 1)
    back = lax.broadcasted_iota(jnp.int32, (n, 2 * n), 0) + HALO - col
    window = (back >= 0) & (back < 8 * WINDOW) & (back % 8 == 0)
    home = c % 2
    slot = 16 * (c // 2)
    for tile in (1, 0):
        lo = tile * n
        allowed = window & ((z > 0) | (col >= HALO)) if tile == 0 else window
        for h in range(HALF // HEAD):
            cols = slice(h * HEAD, (h + 1) * HEAD)
            vcols = slice(HALF + h * HEAD, HALF + (h + 1) * HEAD)
            q = qc[lo : lo + n, cols]
            cot = qc[lo : lo + n, vcols]
            k = k_scr[lo : lo + 2 * n, cols]
            v = v_scr[lo : lo + 2 * n, cols]
            scores = jnp.where(allowed, mm(q, k, 1, 1) * scale, -jnp.inf)
            top = jnp.max(scores, axis=-1, keepdims=True)
            total = jnp.log(jnp.sum(jnp.exp(scores - top), axis=-1, keepdims=True)) + top
            w = jnp.exp(scores - total)
            rounded = w.astype(BF16)
            dp = mm(cot, v, 1, 1)
            spread = jnp.sum(w * dp, axis=-1, keepdims=True)
            ds = (w * (dp - spread) * scale).astype(BF16)
            ag[lo : lo + n, cols] = mm(rounded, v, 1, 0).astype(BF16)
            ag[lo : lo + n, vcols] = mm(ds, k, 1, 0).astype(BF16)
            acc[lo : lo + 2 * n, cols] += mm(ds, q, 0, 0)
            acc[lo : lo + 2 * n, vcols] += mm(rounded, cot, 0, 0)
        for r in range(8):
            d = 8 * tile + (c + r) % 8
            sends.start(
                rows_at(ag, 16 * d, 16), rows_at(rag.at[s], slot, 16), gsem.at[0],
                base + d, home, ((home == s) & (d == c)) if r == 0 else None,
            )
    g[...] = acc[...].astype(BF16)

    def c_view(r, h):
        return wc.at[r % NZ, pl.ds(2 * h, 2)]

    def c_make(r):
        wc[r] = mm(rt[zi[r]].reshape(256, ALL), g[:, HALF:], 1, 0).astype(BF16).reshape(
            4, 4, 16, HALF
        )

    def c_step(k):
        for way, h, length, first in CHAINS:
            if k >= length:
                continue
            own = c_view(way * (length - k), h)
            src = own
            if k > 0:
                src = cb.at[first + k - 1]
                await_bytes(src, csem.at[first + k - 1])

                def add(i, _):
                    src[i] = (src[i].astype(F32) + own[i].astype(F32)).astype(BF16)
                    return 0

                lax.fori_loop(0, 2, add, 0)
            sends.start(src, cb.at[first + k], csem.at[first + k], nxt if way == 1 else prv, s)

    def ab_make(out, r, lhs, lo):
        v = mm(lhs.reshape(512, ALL), g[:, lo : lo + 256], 1, 0).astype(BF16)
        for t in range(NQ):
            out[t, r] = v[:, 128 * t : 128 * t + 128].reshape(8, 4, 16, 128)

    up_x, down_x = (base + y * 4 + xi[1], s), (base + y * 4 + xi[3], s)
    up_y, down_y = (base + yi[1] * 4 + x, s), (base + yi[3] * 4 + x, s)
    plane_rings, line_rings = [], []
    for t in range(2 * NQ):
        part, q = t // NQ, t % NQ
        own = (wa, wb)[part].at[q]
        mid = plane_out.at[t]
        over = (yi, xi)[part]
        plane_rings.append(Ring4(
            sends, lambda r, h, own=own: own.at[r, pl.ds(4 * h, 4)],
            *((up_x, down_x), (up_y, down_y))[part],
            (ring_up.at[t], ring_down.at[t], ring_below.at[t], ring_above.at[t]),
            r1sem.at[t], mid,
        ))
        line_rings.append(Ring4(
            sends, lambda r, h, mid=mid, over=over: mid.at[pl.ds(4 * h, 4), over[r]],
            *((up_y, down_y), (up_x, down_x))[part],
            (ring2_up.at[t], ring2_down.at[t], ring2_below.at[t], ring2_above.at[t]),
            r2sem.at[t], z_out.at[t],
        ))

    def a_make(r):
        ab_make(wa, r, rt[:, :, xi[r]], 0)

    def b_make(r):
        ab_make(wb, r, rt[:, yi[r]], 256)

    for r in (4, 3, 5):
        c_make(r)
    c_step(0)
    a_make(2)
    plane_rings[0].first()
    b_make(2)
    plane_rings[2].first()
    plane_rings[1].first()
    plane_rings[3].first()
    a_make(1)
    a_make(3)
    plane_rings[0].direct()
    b_make(1)
    b_make(3)
    plane_rings[2].direct()
    plane_rings[1].direct()
    plane_rings[3].direct()
    for r in (2, 6, 1, 7, 0):
        c_make(r)
    a_make(0)
    b_make(0)

    def gf_make(lo, count):
        gfp[lo : lo + count, :] = (
            mm(g[lo : lo + count, :HALF], kw[...], 1, 1)
            + mm(g[lo : lo + count, HALF:], vw[...], 1, 1)
        ).astype(BF16)

    def gf_cross(i):
        sends.start(
            rows_at(gfp, 128 * i + 64 * (1 - s), 64), gx.at[pl.ds(64 * i, 64)],
            gsem.at[1 + i], base + c, 1 - s,
        )

    def gf_add(i):
        await_bytes(gx.at[pl.ds(64 * i, 64)], gsem.at[1 + i])

        def add(t, _):
            there = pl.ds(pl.multiple_of(64 * i + 16 * t, 16), 16)
            here = pl.ds(pl.multiple_of(128 * i + 64 * s + 16 * t, 16), 16)
            gx[there] = (gx[there].astype(F32) + gfp[here].astype(F32)).astype(BF16)
            return 0

        lax.fori_loop(0, 4, add, 0)

    def gf_home(i):
        for r in range(4):
            t = (c + r) % 4
            d = 8 * (i - 1) + 4 * s + t
            sends.start(
                rows_at(gx, 64 * i + 16 * t, 16), rows_at(rgf, slot, 16), gsem.at[5],
                base + d, home, ((d == c) & (home == s)) if r == 0 else None,
            )

    gf_make(0, HALO)
    gf_cross(0)
    gf_make(HALO, OWN)
    gf_cross(1)
    gf_cross(2)
    gf_add(0)
    sends.start(gx.at[pl.ds(0, 64)], gh, gsem.at[4], prv, s)
    c_step(1)
    for t in (0, 2, 1, 3):
        plane_rings[t].second()
    gf_add(1)
    gf_home(1)
    gf_add(2)
    c_step(2)
    await_bytes(gh, gsem.at[4])

    def add_halo(t, _):
        there = pl.ds(pl.multiple_of(128 + 16 * t, 16), 16)
        here = pl.ds(pl.multiple_of(16 * t, 16), 16)
        gx[there] = (gx[there].astype(F32) + gh[here].astype(F32)).astype(BF16)
        return 0

    lax.fori_loop(0, 4, add_halo, 0)
    gf_home(2)
    for t in (0, 2, 1, 3):
        plane_rings[t].third()
        line_rings[t].first()
        line_rings[t].direct()
    c_step(3)
    for t in (0, 2, 1, 3):
        line_rings[t].second()
    for t in (0, 2, 1, 3):
        line_rings[t].third()
    for r in range(1, NZ):
        sends.start(z_out.at[:, zi[r]], z_in.at[r - 1], endsem.at[0], zi[r] * PLANE + c, s)
    for way, h, length, first in CHAINS:
        await_bytes(cb.at[first + length - 1], csem.at[first + length - 1])
    for h, (p, m) in enumerate(((3, 13), (10, 7))):
        own = c_view(0, h)

        def add(i, _):
            rc[2 * h + i] = (
                own[i].astype(F32) + cb[p, i].astype(F32) + cb[m, i].astype(F32)
            ).astype(BF16)
            return 0

        lax.fori_loop(0, 2, add, 0)
    for r in range(1, PLANE):
        yy, xx = yi[r // 4], xi[r % 4]
        sends.start(rc.at[yy, xx], cc.at[r - 1], endsem.at[1], base + yy * 4 + xx, s)

    def unpack(value):
        v = value.astype(F32)
        return (
            jnp.concatenate([v[0:8], v[16:24]], axis=0).astype(BF16),
            jnp.concatenate([v[8:16], v[24:32]], axis=0).astype(BF16),
        )

    await_bytes(rag, gsem.at[0])
    for core in range(2):
        for out, at in ((att_out, 0), (gq_out, HALF)):
            for t in range(4):
                for fr, v in enumerate(unpack(rag[core, 32 * t : 32 * t + 32, at : at + HALF])):
                    out[fr, 16 * t : 16 * t + 16, HALF * core : HALF * core + HALF] = v
    await_bytes(rgf, gsem.at[5])
    for t in range(4):
        for fr, v in enumerate(unpack(rgf[32 * t : 32 * t + 32, :])):
            gf_out[fr, 16 * t : 16 * t + 16, :] = v

    await_bytes(z_in, endsem.at[0])
    for t in range(2 * NQ):
        gk_out[:, 128 * t : 128 * t + 128] = lax.fori_loop(
            0, NZ - 1, lambda i, v: v + z_in[i, t].astype(F32), z_out[t, z].astype(F32)
        )
    await_bytes(cc, endsem.at[1])
    gv_out[...] = lax.fori_loop(
        0, PLANE - 1, lambda i, v: v + cc[i].astype(F32), rc[y, x].astype(F32)
    )
    sends.finish()


def shards(features, queries, cotangent, key_weight, value_weight):
    def vm(*shape, dtype=BF16):
        return pltpu.VMEM(shape, dtype)

    sem = pltpu.SemaphoreType.DMA
    t = 2 * NQ
    scratch = [
        vm(D, HALF), vm(D, HALF), vm(128, D), vm(2, 128, 2 * HALF),
        vm(ALL, D), vm(OWN, 2 * HALF), vm(8, 4, 4, 16, ALL),
        vm(ALL, HALF), vm(ALL, HALF), vm(ALL, 2 * HALF, dtype=F32), vm(ALL, 2 * HALF),
        vm(OWN, 2 * HALF), vm(ALL, D), vm(2, 128, 2 * HALF), vm(128, D),
        vm(192, D), vm(64, D),
        vm(NQ, 4, 8, 4, 16, 128), vm(NQ, 4, 8, 4, 16, 128), vm(8, 4, 4, 16, HALF),
        vm(t, 4, 4, 16, 128), vm(t, 4, 4, 16, 128), vm(t, 8, 4, 16, 128), vm(t, 8, 4, 16, 128),
        vm(t, 8, 4, 16, 128),
        vm(t, 4, 16, 128), vm(t, 4, 16, 128), vm(t, 8, 16, 128), vm(t, 8, 16, 128),
        vm(t, 8, 16, 128), vm(NZ - 1, t, 16, 128),
        vm(14, 2, 4, 16, HALF), vm(4, 4, 16, HALF), vm(PLANE - 1, 16, HALF),
        sem((160,)), sem((2,)), sem((4,)), sem((16,)), sem((8,)), sem((6,)),
        sem((t, 6)), sem((t, 6)), sem((14,)), sem((2,)),
    ]
    vmem = pl.BlockSpec(memory_space=pltpu.VMEM)
    hbm = pl.BlockSpec(memory_space=pl.ANY)
    return pl.pallas_call(
        kernel,
        out_shape=(
            jax.ShapeDtypeStruct(queries.shape, BF16),
            jax.ShapeDtypeStruct(features.shape, BF16),
            jax.ShapeDtypeStruct(queries.shape, BF16),
            jax.ShapeDtypeStruct((16, HALF), F32),
            jax.ShapeDtypeStruct((16, HALF), F32),
        ),
        in_specs=[vmem, vmem, vmem, hbm, hbm],
        out_specs=[vmem] * 5,
        scratch_shapes=scratch,
        compiler_params=pltpu.CompilerParams(
            collective_id=0, has_side_effects=True, vmem_limit_bytes=52 * MIB
        ),
    )(features, queries, cotangent, key_weight, value_weight)


def solution(mesh):
    rows = P("tm", "space", None)
    return jax.shard_map(
        shards,
        mesh=mesh,
        in_specs=(rows, rows, rows, P(None, "space"), P(None, "space")),
        out_specs=(rows, rows, rows, P("tm", "space"), P("tm", "space")),
        check_vma=False,
    )
```

```python
import jax
import jax.numpy as jnp
from jax import lax
from jax.experimental import pallas as pl
from jax.experimental.pallas import tpu as pltpu
from jax.sharding import PartitionSpec as P

HEAD = 128
WINDOW = 16
PLANE = 16
NZ = 8
OWN = 256
HALO = 128
ALL = HALO + OWN
HALF = 512
D = 2048
F32 = jnp.float32
BF16 = jnp.bfloat16
MIB = 2**20


def mm(a, b, ca, cb):
    return lax.dot_general(a, b, (((ca,), (cb,)), ((), ())), preferred_element_type=F32)


def rows_at(ref, start, count):
    return ref.at[pl.ds(pl.multiple_of(start, 16), count)]


def signal(sem, tm, core):
    pl.semaphore_signal(
        sem, inc=1, device_id=(tm, core), device_id_type=pl.DeviceIdType.MESH
    )


def await_bytes(ref, sem):
    pltpu.make_async_copy(ref, ref, sem).wait()


class Sends:
    def __init__(self, sems):
        self.sems, self.used, self.waits = sems, 0, []

    def start(self, src, dst, rsem, tm, core, self_if=None):
        copy = pltpu.make_async_remote_copy(
            src_ref=src, dst_ref=dst, send_sem=self.sems.at[self.used], recv_sem=rsem,
            device_id=(tm, core), device_id_type=pl.DeviceIdType.MESH,
        )
        self.used += 1
        if self_if is None:
            copy.start()
        else:
            pl.when(self_if)(lambda: pltpu.make_async_copy(src, dst, rsem).start())
            pl.when(jnp.logical_not(self_if))(copy.start)
        self.waits.append((copy, self_if))

    def settle(self, i):
        if self.waits[i] is None:
            return
        copy, self_if = self.waits[i]
        self.waits[i] = None
        if self_if is None:
            copy.wait_send()
        else:
            pl.when(jnp.logical_not(self_if))(copy.wait_send)

    def finish(self):
        for i in range(self.used):
            self.settle(i)


class Ring4:
    def __init__(self, sends, view, up, down, bufs, sems, out):
        self.sends, self.view, self.up, self.down = sends, view, up, down
        self.bufs, self.sems, self.out = bufs, sems, out

    def first(self):
        self.sends.start(self.view(2, 0), self.bufs[0], self.sems.at[0], *self.up)
        self.sends.start(self.view(2, 1), self.bufs[1], self.sems.at[1], *self.down)

    def direct(self):
        _, _, below, above = self.bufs
        h = below.shape[0] // 2
        self.sends.start(self.view(1, 1), below.at[pl.ds(h, h)], self.sems.at[2], *self.up)
        self.sends.start(self.view(3, 0), above.at[pl.ds(0, h)], self.sems.at[3], *self.down)

    def second(self):
        from_below, from_above, below, above = self.bufs
        h = below.shape[0] // 2
        for buf, sem, view, dst, dsem, dev in (
            (from_below, 0, self.view(1, 0), below.at[pl.ds(0, h)], 4, self.up),
            (from_above, 1, self.view(3, 1), above.at[pl.ds(h, h)], 5, self.down),
        ):
            await_bytes(buf, self.sems.at[sem])

            def add(i, _):
                buf[i] = (buf[i].astype(F32) + view[i].astype(F32)).astype(BF16)
                return 0

            lax.fori_loop(0, h, add, 0)
            self.sends.start(buf, dst, self.sems.at[dsem], *dev)

    def third(self):
        _, _, below, above = self.bufs
        h = below.shape[0] // 2
        await_bytes(below.at[pl.ds(h, h)], self.sems.at[2])
        await_bytes(above.at[pl.ds(0, h)], self.sems.at[3])
        await_bytes(below.at[pl.ds(0, h)], self.sems.at[4])
        await_bytes(above.at[pl.ds(h, h)], self.sems.at[5])
        for half in range(2):
            own = self.view(0, half)

            def add(i, _):
                j = half * h + i
                self.out[j] = (
                    own[i].astype(F32) + below[j].astype(F32) + above[j].astype(F32)
                ).astype(BF16)
                return 0

            lax.fori_loop(0, h, add, 0)


NA, NB = 2, 2
NT = NA + NB
CW = 1024 - 128 * NT
ORDER = (
    "p01", "p00", "T0", "B0", "a0", "p10", "gfH", "p11", "F", "gf0", "T1", "gf", "c26", "B1",
    "S0", "S2", "S1", "S3", "a1", "c170", "T2", "H0", "H2", "H1", "H3", "home1", "home2", "B2",
    "L0", "L2", "L1", "L3", "T3", "att", "M0", "M2", "M1", "M3", "Z", "gfout", "C",
)
CHAINS = ((1, 0, 4, 0), (-1, 1, 4, 4), (1, 1, 3, 8), (-1, 0, 3, 11))


def kernel(
    f_hbm, q_hbm, c_hbm, kw_hbm, vw_hbm,
    att_out, gf_out, gq_out, gk_out, gv_out,
    f_ref, q_ref, c_ref, kw, vw, fb, qcb, rows, qc, rt, k_scr, v_scr, acc, g, ag, gfp, rag, rgf, gx, gh,
    wa, wb, wc, ring_up, ring_down, ring_below, ring_above, plane_out,
    ring2_up, ring2_down, ring2_below, ring2_above, z_out, z_in, cb, rc, cc,
    send, wsem, got, qsem, fsem, hsem, gsem, r1sem, r2sem, csem, endsem,
):
    tm = lax.axis_index("tm")
    s = lax.axis_index("space")
    z, c = tm // PLANE, tm % PLANE
    y, x = c // 4, c % 4
    base = z * PLANE
    zi = [(z + r) % NZ for r in range(NZ)]
    yi = [(y + r) % 4 for r in range(4)]
    xi = [(x + r) % 4 for r in range(4)]
    nxt, prv = zi[1] * PLANE + c, zi[7] * PLANE + c

    loads = [
        pltpu.make_async_copy(src, dst, wsem.at[i])
        for i, (src, dst) in enumerate(
            ((f_hbm, f_ref), (q_hbm, q_ref), (c_hbm, c_ref), (kw_hbm, kw), (vw_hbm, vw))
        )
    ]
    loads[0].start()
    barrier = pltpu.get_barrier_semaphore()
    for r in range(1, PLANE):
        for core in range(2):
            signal(barrier, base + (c + r) % PLANE, core)
    signal(barrier, base + c, 1 - s)
    for r in range(1, NZ):
        signal(barrier, zi[r] * PLANE + c, s)

    def pack(ref, out, cols, at):
        w = cols[1] - cols[0]
        for t in range(4):
            p, q = (ref[i, 16 * t : 16 * t + 16, cols[0] : cols[1]].astype(F32) for i in range(2))
            out[32 * t : 32 * t + 32, at : at + w] = jnp.concatenate(
                [p[:8], q[:8], p[8:], q[8:]], axis=0
            ).astype(BF16)

    for copy in loads[1:]:
        copy.start()
    loads[0].wait()
    pack(f_ref, fb, (0, D), 0)
    pl.semaphore_wait(barrier, 2 * (PLANE - 1) + 1 + NZ - 1)

    sends = Sends(send)
    home = c % 2
    slot = 16 * (c // 2)
    to = (c // 4) % 2
    mine = c % 2 == s
    for r in range(8):
        j = (c // 2 + r) % 8
        sends.start(
            rows_at(fb, 16 * j, 16), rows_at(rows, HALO + 16 * c, 16), fsem.at[c],
            base + 2 * j + s, to, (mine & (to == s)) if r == 0 else None,
        )
    loads[1].wait()
    loads[2].wait()
    for pair in range(2):
        for core in range(2):
            at = HALF * core + 256 * pair
            pack(q_ref, qcb.at[core, pair], (at, at + 256), 0)
            pack(c_ref, qcb.at[core, pair], (at, at + 256), 256)
    for pair in range(2):
        for r in range(8):
            j = (c // 2 + r) % 8
            if pair == 0:
                sends.settle(r)
            for o in range(2):
                core = (s + o) % 2
                sends.start(
                    rows_at(qcb.at[core, pair], 16 * j, 16), rows_at(qc.at[pair], 16 * c, 16),
                    qsem.at[pair], base + 2 * j + s, core, mine if r == 0 and o == 0 else None,
                )
    for r in range(4):
        i = 4 * s + xi[r]
        block = rows_at(rows, HALO + 128 + 16 * i, 16)
        await_bytes(block, fsem.at[8 + i])
        sends.start(block, rows_at(rows, 16 * i, 16), hsem.at[i], nxt, s)
        sends.start(block, block, got.at[0], base + c, 1 - s)
    for r in range(4):
        i = 4 * s + xi[r]
        block = rows_at(rows, HALO + 16 * i, 16)
        await_bytes(block, fsem.at[i])
        sends.start(block, block, got.at[1], base + c, 1 - s)

    def project(lo):
        part = rows[lo : lo + 128, :]
        k_scr[lo : lo + 128, :] = mm(part, kw[...], 1, 0).astype(BF16)
        v_scr[lo : lo + 128, :] = mm(part, vw[...], 1, 0).astype(BF16)
        rt[:, :, :, :, lo : lo + 128] = part.T.reshape(8, 4, 4, 16, 128)

    def other(lo):
        return rows_at(rows, lo + 64 * (1 - s), 64)

    loads[3].wait()
    loads[4].wait()
    await_bytes(other(HALO + 128), got.at[0])
    project(HALO + 128)
    await_bytes(other(HALO), got.at[1])
    project(HALO)
    acc[...] = jnp.zeros_like(acc)

    def gf_make(lo, count):
        gfp[lo : lo + count, :] = (
            mm(g[lo : lo + count, 0:256], kw[:, 0:256], 1, 1)
            + mm(g[lo : lo + count, 256:512], vw[:, 0:256], 1, 1)
            + mm(g[lo : lo + count, 512:768], kw[:, 256:512], 1, 1)
            + mm(g[lo : lo + count, 768:1024], vw[:, 256:512], 1, 1)
        ).astype(BF16)

    def gf_cross(i):
        sends.start(
            rows_at(gfp, 128 * i + 64 * (1 - s), 64), gx.at[pl.ds(64 * i, 64)],
            gsem.at[1 + i], base + c, 1 - s,
        )

    def gf_add(i):
        await_bytes(gx.at[pl.ds(64 * i, 64)], gsem.at[1 + i])

        def add(t, _):
            there = pl.ds(pl.multiple_of(64 * i + 16 * t, 16), 16)
            here = pl.ds(pl.multiple_of(128 * i + 64 * s + 16 * t, 16), 16)
            gx[there] = (gx[there].astype(F32) + gfp[here].astype(F32)).astype(BF16)
            return 0

        lax.fori_loop(0, 4, add, 0)

    def gf_home(i):
        for r in range(4):
            t = (c + r) % 4
            d = 8 * (i - 1) + 4 * s + t
            sends.start(
                rows_at(gx, 64 * i + 16 * t, 16), rows_at(rgf, slot, 16), gsem.at[5],
                base + d, home, ((d == c) & (home == s)) if r == 0 else None,
            )

    scale = HEAD ** -0.5
    n = OWN // 2
    col = lax.broadcasted_iota(jnp.int32, (n, 2 * n), 1)
    back = lax.broadcasted_iota(jnp.int32, (n, 2 * n), 0) + HALO - col
    window = (back >= 0) & (back < 8 * WINDOW) & (back % 8 == 0)
    keep = (window & ((z > 0) | (col >= HALO)), window)

    def attend(pair, tile):
        lo = tile * n
        for h in range(2):
            cols = slice(128 * h, 128 * h + 128)
            vcols = slice(256 + 128 * h, 384 + 128 * h)
            at = 512 * pair + 128 * h
            head = slice(256 * pair + 128 * h, 256 * pair + 128 * h + 128)
            q = qc[pair, lo : lo + n, cols]
            cot = qc[pair, lo : lo + n, vcols]
            k = k_scr[lo : lo + 2 * n, head]
            v = v_scr[lo : lo + 2 * n, head]
            scores = jnp.where(keep[tile], mm(q, k, 1, 1) * scale, -jnp.inf)
            e = jnp.exp(scores - jnp.max(scores, axis=-1, keepdims=True))
            w = e / jnp.sum(e, axis=-1, keepdims=True)
            rounded = w.astype(BF16)
            dp = mm(cot, v, 1, 1)
            spread = jnp.sum(w * dp, axis=-1, keepdims=True)
            ds = (w * (dp - spread) * scale).astype(BF16)
            ag[pair, lo : lo + n, cols] = mm(rounded, v, 1, 0).astype(BF16)
            ag[pair, lo : lo + n, vcols] = mm(ds, k, 1, 0).astype(BF16)
            acc[lo : lo + 2 * n, at : at + 128] += mm(ds, q, 0, 0)
            acc[lo : lo + 2 * n, at + 256 : at + 384] += mm(rounded, cot, 0, 0)

    def ag_home(pair, tile):
        for r in range(8):
            d = 8 * tile + (c + r) % 8
            sends.start(
                rows_at(ag.at[pair], 16 * d, 16), rows_at(rag.at[s, pair], slot, 16), gsem.at[0],
                base + d, home, ((home == s) & (d == c)) if r == 0 else None,
            )

    def c_view(r, h):
        return wc.at[r % NZ, pl.ds(2 * h, 2)]

    def c_make(*steps):
        for r in steps:
            wc[r] = mm(rt[zi[r]].reshape(256, ALL), g[:, :CW], 1, 0).astype(BF16).reshape(
                4, 4, 16, CW
            )

    def c_step(chains, k):
        for way, h, length, first in chains:
            own = c_view(way * (length - k), h)
            src = own
            if k > 0:
                src = cb.at[first + k - 1]
                await_bytes(src, csem.at[first + k - 1])

                def add(i, _):
                    src[i] = (src[i].astype(F32) + own[i].astype(F32)).astype(BF16)
                    return 0

                lax.fori_loop(0, 2, add, 0)
            sends.start(src, cb.at[first + k], csem.at[first + k], nxt if way == 1 else prv, s)

    def ab_make(out, r, lhs, lo, count):
        v = mm(lhs.reshape(512, ALL), g[:, lo : lo + 128 * count], 1, 0).astype(BF16)
        for t in range(count):
            out[t, r] = v[:, 128 * t : 128 * t + 128].reshape(8, 4, 16, 128)

    up_x, down_x = (base + y * 4 + xi[1], s), (base + y * 4 + xi[3], s)
    up_y, down_y = (base + yi[1] * 4 + x, s), (base + yi[3] * 4 + x, s)
    plane_rings, line_rings = [], []
    for t in range(NT):
        part, q = (0, t) if t < NA else (1, t - NA)
        own = (wa, wb)[part].at[q]
        mid = plane_out.at[t]
        over = (yi, xi)[part]
        plane_rings.append(Ring4(
            sends, lambda r, h, own=own: own.at[r, pl.ds(4 * h, 4)],
            *((up_x, down_x), (up_y, down_y))[part],
            (ring_up.at[t], ring_down.at[t], ring_below.at[t], ring_above.at[t]),
            r1sem.at[t], mid,
        ))
        line_rings.append(Ring4(
            sends, lambda r, h, mid=mid, over=over: mid.at[pl.ds(4 * h, 4), over[r]],
            *((up_y, down_y), (up_x, down_x))[part],
            (ring2_up.at[t], ring2_down.at[t], ring2_below.at[t], ring2_above.at[t]),
            r2sem.at[t], z_out.at[t],
        ))

    def a_make(r):
        ab_make(wa, r, rt[:, :, xi[r]], CW, NA)

    def b_make(r):
        ab_make(wb, r, rt[:, yi[r]], CW + 128 * NA, NB)

    def ring_start():
        a_make(2)
        for t in range(NA):
            plane_rings[t].first()
        b_make(2)
        for t in range(NA, NT):
            plane_rings[t].first()
        a_make(1)
        a_make(3)
        for t in range(NA):
            plane_rings[t].direct()
        b_make(1)
        b_make(3)
        for t in range(NA, NT):
            plane_rings[t].direct()

    def c_first():
        c_make(4)
        c_step(CHAINS[:2], 0)

    def c_second():
        c_make(3, 5)
        c_step(CHAINS[2:], 0)

    def gf_own():
        gf_make(HALO, OWN)
        gf_cross(1)
        gf_cross(2)

    def gf_home1():
        gf_add(1)
        gf_home(1)

    def gf_home2():
        gf_add(2)
        await_bytes(gh, gsem.at[4])

        def add_halo(t, _):
            there = pl.ds(pl.multiple_of(128 + 16 * t, 16), 16)
            here = pl.ds(pl.multiple_of(16 * t, 16), 16)
            gx[there] = (gx[there].astype(F32) + gh[here].astype(F32)).astype(BF16)
            return 0

        lax.fori_loop(0, 4, add_halo, 0)
        gf_home(2)

    def own_slices():
        c_make(1, 7, 0)
        a_make(0)
        b_make(0)

    def to_line(t):
        plane_rings[t].third()
        line_rings[t].first()
        line_rings[t].direct()

    def unpack(value):
        v = value.astype(F32)
        return (
            jnp.concatenate([v[0:8], v[16:24]], axis=0).astype(BF16),
            jnp.concatenate([v[8:16], v[24:32]], axis=0).astype(BF16),
        )

    def att_unpack():
        await_bytes(rag, gsem.at[0])
        for core in range(2):
            for pair in range(2):
                to = HALF * core + 256 * pair
                for out, at in ((att_out, 0), (gq_out, 256)):
                    for t in range(4):
                        part = rag[core, pair, 32 * t : 32 * t + 32, at : at + 256]
                        for fr, v in enumerate(unpack(part)):
                            out[fr, 16 * t : 16 * t + 16, to : to + 256] = v

    def gf_unpack():
        await_bytes(rgf, gsem.at[5])
        for t in range(4):
            for fr, v in enumerate(unpack(rgf[32 * t : 32 * t + 32, :])):
                gf_out[fr, 16 * t : 16 * t + 16, :] = v

    def z_sends():
        for r in range(1, NZ):
            sends.start(z_out.at[:, zi[r]], z_in.at[r - 1], endsem.at[0], zi[r] * PLANE + c, s)

    def c_last():
        for way, h, length, first in CHAINS:
            await_bytes(cb.at[first + length - 1], csem.at[first + length - 1])
        for h, (p, m) in enumerate(((3, 13), (10, 7))):
            own = c_view(0, h)

            def add(i, _):
                rc[2 * h + i] = (
                    own[i].astype(F32) + cb[p, i].astype(F32) + cb[m, i].astype(F32)
                ).astype(BF16)
                return 0

            lax.fori_loop(0, 2, add, 0)
        for r in range(1, PLANE):
            yy, xx = yi[r // 4], xi[r % 4]
            sends.start(rc.at[yy, xx], cc.at[r - 1], endsem.at[1], base + yy * 4 + xx, s)

    def halo_relay():
        for r in range(4):
            i = 4 * s + xi[r]
            block = rows_at(rows, 16 * i, 16)
            await_bytes(block, hsem.at[i])
            sends.start(block, block, got.at[2], base + c, 1 - s)

    def first_heads(tile):
        if tile == 1:
            await_bytes(qc.at[0], qsem.at[0])
        else:
            halo_relay()
            await_bytes(other(0), got.at[2])
            project(0)
        attend(0, tile)
        if tile == 0:
            g[:, :512] = acc[:, :512].astype(BF16)

    def second_heads(tile):
        if tile == 0:
            await_bytes(qc.at[1], qsem.at[1])
        attend(1, tile)
        if tile == 1:
            g[HALO:, 512:] = acc[HALO:, 512:].astype(BF16)

    def gf_halo():
        g[:HALO, 512:] = acc[:HALO, 512:].astype(BF16)
        gf_make(0, HALO)
        gf_cross(0)

    def gf_back():
        gf_add(0)
        sends.start(gx.at[pl.ds(0, 64)], gh, gsem.at[4], prv, s)

    steps = {
        "p01": lambda: first_heads(1), "p00": lambda: first_heads(0),
        "p10": lambda: second_heads(0), "p11": lambda: second_heads(1),
        "a0": lambda: (ag_home(0, 1), ag_home(0, 0)), "a1": lambda: (ag_home(1, 0), ag_home(1, 1)),
        "gfH": gf_halo, "gf0": gf_back,
        "T0": c_first, "B0": c_second, "F": ring_start, "gf": gf_own, "home1": gf_home1,
        "home2": gf_home2, "c26": lambda: c_make(2, 6), "c170": own_slices,
        "att": att_unpack, "gfout": gf_unpack, "Z": z_sends, "C": c_last,
    }
    for k in range(1, 4):
        steps["T%d" % k] = lambda k=k: c_step(CHAINS[:2], k)
        steps["B%d" % k] = lambda k=k: c_step(CHAINS[2:], k)
    for t in range(NT):
        steps["S%d" % t] = plane_rings[t].second
        steps["H%d" % t] = lambda t=t: to_line(t)
        steps["L%d" % t] = line_rings[t].second
        steps["M%d" % t] = line_rings[t].third
    for name in ORDER:
        steps[name]()

    await_bytes(z_in, endsem.at[0])
    for t in range(NT):
        out, at = (gk_out, 256 + 128 * t) if t < NA else (gv_out, 256 + 128 * (t - NA))
        out[:, at : at + 128] = lax.fori_loop(
            0, NZ - 1, lambda i, v: v + z_in[i, t].astype(F32), z_out[t, z].astype(F32)
        )
    await_bytes(cc, endsem.at[1])
    last = lax.fori_loop(
        0, PLANE - 1, lambda i, v: v + cc[i].astype(F32), rc[y, x].astype(F32)
    )
    gk_out[:, 0:256] = last[:, 0:256]
    gv_out[:, 0:256] = last[:, 256:512]
    sends.finish()


def leave_kernel(*refs):
    into, out = (
        [pltpu.make_async_copy(src[i], dst[i], sem.at[i]) for i in range(5)]
        for src, dst, sem in ((refs[0:5], refs[10:15], refs[15]), (refs[10:15], refs[5:10], refs[16]))
    )
    for copy in into:
        copy.start()
    for i in range(5):
        into[i].wait()
        out[i].start()
    for copy in out:
        copy.wait()


def shards(features, queries, cotangent, key_weight, value_weight):
    def vm(*shape, dtype=BF16):
        return pltpu.VMEM(shape, dtype)

    sem = pltpu.SemaphoreType.DMA
    t = NT
    scratch = [
        vm(2, 64, D), vm(2, 64, 2 * HALF), vm(2, 64, 2 * HALF),
        vm(D, HALF), vm(D, HALF), vm(128, D), vm(2, 2, 128, HALF),
        vm(ALL, D), vm(2, OWN, HALF), vm(8, 4, 4, 16, ALL),
        vm(ALL, HALF), vm(ALL, HALF), vm(ALL, 2 * HALF, dtype=F32), vm(ALL, 2 * HALF),
        vm(2, OWN, HALF), vm(ALL, D), vm(2, 2, 128, HALF), vm(128, D),
        vm(192, D), vm(64, D),
        vm(NA, 4, 8, 4, 16, 128), vm(NB, 4, 8, 4, 16, 128), vm(8, 4, 4, 16, CW),
        vm(t, 4, 4, 16, 128), vm(t, 4, 4, 16, 128), vm(t, 8, 4, 16, 128), vm(t, 8, 4, 16, 128),
        vm(t, 8, 4, 16, 128),
        vm(t, 4, 16, 128), vm(t, 4, 16, 128), vm(t, 8, 16, 128), vm(t, 8, 16, 128),
        vm(t, 8, 16, 128), vm(NZ - 1, t, 16, 128),
        vm(14, 2, 4, 16, CW), vm(4, 4, 16, CW), vm(PLANE - 1, 16, CW),
        sem((200,)), sem((5,)), sem((3,)), sem((2,)), sem((16,)), sem((8,)), sem((6,)),
        sem((t, 6)), sem((t, 6)), sem((14,)), sem((2,)),
    ]
    vmem = pl.BlockSpec(memory_space=pltpu.VMEM)
    hbm = pl.BlockSpec(memory_space=pl.ANY)
    results = pl.pallas_call(
        kernel,
        out_shape=(
            jax.ShapeDtypeStruct(queries.shape, BF16),
            jax.ShapeDtypeStruct(features.shape, BF16),
            jax.ShapeDtypeStruct(queries.shape, BF16),
            jax.ShapeDtypeStruct((16, HALF), F32),
            jax.ShapeDtypeStruct((16, HALF), F32),
        ),
        in_specs=[hbm] * 5,
        out_specs=[vmem] * 5,
        scratch_shapes=scratch,
        compiler_params=pltpu.CompilerParams(
            collective_id=0, has_side_effects=True, vmem_limit_bytes=61 * MIB
        ),
    )(features, queries, cotangent, key_weight, value_weight)
    return pl.pallas_call(
        leave_kernel,
        out_shape=tuple(jax.ShapeDtypeStruct(v.shape, v.dtype) for v in results),
        in_specs=[hbm] * 5,
        out_specs=[hbm] * 5,
        scratch_shapes=[pltpu.VMEM(v.shape, v.dtype) for v in results] + [sem((5,)), sem((5,))],
        compiler_params=pltpu.CompilerParams(vmem_limit_bytes=61 * MIB),
    )(*results)


def solution(mesh):
    rows = P("tm", "space", None)
    return jax.shard_map(
        shards,
        mesh=mesh,
        in_specs=(rows, rows, rows, P(None, "space"), P(None, "space")),
        out_specs=(rows, rows, rows, P("tm", "space"), P("tm", "space")),
        check_vma=False,
    )
```

```python
import jax
import jax.numpy as jnp
from jax import lax
from jax.experimental import pallas as pl
from jax.experimental.pallas import tpu as pltpu
from jax.sharding import PartitionSpec as P

HEAD = 128
WINDOW = 16
PLANE = 16
NZ = 8
OWN = 256
HALO = 128
ALL = HALO + OWN
HALF = 512
D = 2048
F32 = jnp.float32
BF16 = jnp.bfloat16
MIB = 2**20


def mm(a, b, ca, cb):
    return lax.dot_general(a, b, (((ca,), (cb,)), ((), ())), preferred_element_type=F32)


def rows_at(ref, start, count):
    return ref.at[pl.ds(pl.multiple_of(start, 16), count)]


def signal(sem, tm, core):
    pl.semaphore_signal(
        sem, inc=1, device_id=(tm, core), device_id_type=pl.DeviceIdType.MESH
    )


def await_bytes(ref, sem):
    pltpu.make_async_copy(ref, ref, sem).wait()


class Sends:
    def __init__(self, sems):
        self.sems, self.used, self.waits = sems, 0, []

    def start(self, src, dst, rsem, tm, core, self_if=None):
        copy = pltpu.make_async_remote_copy(
            src_ref=src, dst_ref=dst, send_sem=self.sems.at[self.used], recv_sem=rsem,
            device_id=(tm, core), device_id_type=pl.DeviceIdType.MESH,
        )
        self.used += 1
        if self_if is None:
            copy.start()
        else:
            pl.when(self_if)(lambda: pltpu.make_async_copy(src, dst, rsem).start())
            pl.when(jnp.logical_not(self_if))(copy.start)
        self.waits.append((copy, self_if))

    def settle(self, i):
        if self.waits[i] is None:
            return
        copy, self_if = self.waits[i]
        self.waits[i] = None
        if self_if is None:
            copy.wait_send()
        else:
            pl.when(jnp.logical_not(self_if))(copy.wait_send)

    def finish(self):
        for i in range(self.used):
            self.settle(i)


class Ring4:
    def __init__(self, sends, view, up, down, bufs, sems, out):
        self.sends, self.view, self.up, self.down = sends, view, up, down
        self.bufs, self.sems, self.out = bufs, sems, out

    def first(self):
        self.sends.start(self.view(2, 0), self.bufs[0], self.sems.at[0], *self.up)
        self.sends.start(self.view(2, 1), self.bufs[1], self.sems.at[1], *self.down)

    def direct(self):
        _, _, below, above = self.bufs
        h = below.shape[0] // 2
        self.sends.start(self.view(1, 1), below.at[pl.ds(h, h)], self.sems.at[2], *self.up)
        self.sends.start(self.view(3, 0), above.at[pl.ds(0, h)], self.sems.at[3], *self.down)

    def second(self):
        from_below, from_above, below, above = self.bufs
        h = below.shape[0] // 2
        for buf, sem, view, dst, dsem, dev in (
            (from_below, 0, self.view(1, 0), below.at[pl.ds(0, h)], 4, self.up),
            (from_above, 1, self.view(3, 1), above.at[pl.ds(h, h)], 5, self.down),
        ):
            await_bytes(buf, self.sems.at[sem])

            def add(i, _):
                buf[i] = (buf[i].astype(F32) + view[i].astype(F32)).astype(BF16)
                return 0

            lax.fori_loop(0, h, add, 0)
            self.sends.start(buf, dst, self.sems.at[dsem], *dev)

    def third(self):
        _, _, below, above = self.bufs
        h = below.shape[0] // 2
        await_bytes(below.at[pl.ds(h, h)], self.sems.at[2])
        await_bytes(above.at[pl.ds(0, h)], self.sems.at[3])
        await_bytes(below.at[pl.ds(0, h)], self.sems.at[4])
        await_bytes(above.at[pl.ds(h, h)], self.sems.at[5])
        for half in range(2):
            own = self.view(0, half)

            def add(i, _):
                j = half * h + i
                self.out[j] = (
                    own[i].astype(F32) + below[j].astype(F32) + above[j].astype(F32)
                ).astype(BF16)
                return 0

            lax.fori_loop(0, h, add, 0)


NA, NB = 2, 2
NT = NA + NB
CW = 1024 - 128 * NT
ORDER = (
    "p01", "a01", "p00", "T0", "B0", "a00", "p10", "gfH", "p11", "F", "gf0", "T1", "gf", "c26",
    "B1", "S0", "S2", "S1", "S3", "c170", "T2", "H0", "H2", "H1", "H3", "a10", "a11", "home1",
    "home2", "B2", "T3", "M0", "M2", "M1", "M3", "Z", "C", "att", "gfout",
)
class Line4:
    def __init__(self, sends, mine, slices, devices, buf, sem, out):
        self.sends, self.mine, self.slices, self.devices = sends, mine, slices, devices
        self.buf, self.sem, self.out = buf, sem, out

    def start(self):
        for r, (piece, device) in enumerate(zip(self.slices, self.devices)):
            self.sends.start(piece, self.buf.at[r], self.sem, *device)

    def finish(self):
        await_bytes(self.buf, self.sem)

        def add(i, _):
            total = self.mine[i].astype(F32)
            for r in range(3):
                total += self.buf[r, i].astype(F32)
            self.out[i] = total.astype(BF16)
            return 0

        lax.fori_loop(0, NZ, add, 0)


CHAINS = ((1, 0, 4, 0), (-1, 1, 4, 4), (1, 1, 3, 8), (-1, 0, 3, 11))


def kernel(
    f_hbm, q_hbm, c_hbm, kw_hbm, vw_hbm,
    att_hbm, gf_hbm, gq_hbm, gk_hbm, gv_hbm,
    att_out, gf_out, gq_out, gk_out, gv_out,
    f_ref, q_ref, c_ref, kw, vw, fb, qcb, rows, qc, rt, k_scr, v_scr, acc, g, ag, gfp, rag, rgf, gx, gh,
    wa, wb, wc, ring_up, ring_down, ring_below, ring_above, plane_out,
    ring2, z_out, z_in, cb, rc, cc,
    send, wsem, got, qsem, fsem, hsem, gsem, r1sem, r2sem, csem, endsem, osem,
):
    tm = lax.axis_index("tm")
    s = lax.axis_index("space")
    z, c = tm // PLANE, tm % PLANE
    y, x = c // 4, c % 4
    base = z * PLANE
    zi = [(z + r) % NZ for r in range(NZ)]
    yi = [(y + r) % 4 for r in range(4)]
    xi = [(x + r) % 4 for r in range(4)]
    nxt, prv = zi[1] * PLANE + c, zi[7] * PLANE + c

    loads = [
        pltpu.make_async_copy(src, dst, wsem.at[i])
        for i, (src, dst) in enumerate(
            ((q_hbm, q_ref), (c_hbm, c_ref), (kw_hbm, kw), (vw_hbm, vw))
        )
    ]
    f_loads = [
        pltpu.make_async_copy(
            f_hbm.at[:, 16 * t : 16 * t + 16], f_ref.at[:, 16 * t : 16 * t + 16], wsem.at[5 + t]
        )
        for t in range(4)
    ]
    for copy in f_loads:
        copy.start()
    barrier = pltpu.get_barrier_semaphore()
    for r in range(1, PLANE):
        for core in range(2):
            signal(barrier, base + (c + r) % PLANE, core)
    signal(barrier, base + c, 1 - s)
    for r in range(1, NZ):
        signal(barrier, zi[r] * PLANE + c, s)

    def pack(ref, out, cols, at, waits=None):
        w = cols[1] - cols[0]
        for t in range(4):
            if waits:
                waits[t].wait()
            p, q = (ref[i, 16 * t : 16 * t + 16, cols[0] : cols[1]].astype(F32) for i in range(2))
            out[32 * t : 32 * t + 32, at : at + w] = jnp.concatenate(
                [p[:8], q[:8], p[8:], q[8:]], axis=0
            ).astype(BF16)

    for copy in loads:
        copy.start()
    pack(f_ref, fb, (0, D), 0, f_loads)
    pl.semaphore_wait(barrier, 2 * (PLANE - 1) + 1 + NZ - 1)

    sends = Sends(send)
    home = c % 2
    slot = 16 * (c // 2)
    to = (c // 4) % 2
    mine = c % 2 == s
    for r in range(8):
        j = (c // 2 + r) % 8
        sends.start(
            rows_at(fb, 16 * j, 16), rows_at(rows, HALO + 16 * c, 16), fsem.at[c],
            base + 2 * j + s, to, (mine & (to == s)) if r == 0 else None,
        )
    loads[0].wait()
    loads[1].wait()
    for pair in range(2):
        for core in range(2):
            at = HALF * core + 256 * pair
            pack(q_ref, qcb.at[core, pair], (at, at + 256), 0)
            pack(c_ref, qcb.at[core, pair], (at, at + 256), 256)
    for pair in range(2):
        for r in range(8):
            j = (c // 2 + r) % 8
            if pair == 0:
                sends.settle(r)
            for o in range(2):
                core = (s + o) % 2
                sends.start(
                    rows_at(qcb.at[core, pair], 16 * j, 16), rows_at(qc.at[pair], 16 * c, 16),
                    qsem.at[pair], base + 2 * j + s, core, mine if r == 0 and o == 0 else None,
                )
    for r in range(4):
        i = 4 * s + xi[r]
        block = rows_at(rows, HALO + 128 + 16 * i, 16)
        await_bytes(block, fsem.at[8 + i])
        sends.start(block, rows_at(rows, 16 * i, 16), hsem.at[i], nxt, s)
        sends.start(block, block, got.at[0], base + c, 1 - s)
    for r in range(4):
        i = 4 * s + xi[r]
        block = rows_at(rows, HALO + 16 * i, 16)
        await_bytes(block, fsem.at[i])
        sends.start(block, block, got.at[1], base + c, 1 - s)

    def project(lo):
        part = rows[lo : lo + 128, :]
        k_scr[lo : lo + 128, :] = mm(part, kw[...], 1, 0).astype(BF16)
        v_scr[lo : lo + 128, :] = mm(part, vw[...], 1, 0).astype(BF16)
        rt[:, :, :, :, lo : lo + 128] = part.T.reshape(8, 4, 4, 16, 128)

    def other(lo):
        return rows_at(rows, lo + 64 * (1 - s), 64)

    loads[2].wait()
    loads[3].wait()
    await_bytes(other(HALO + 128), got.at[0])
    project(HALO + 128)
    await_bytes(other(HALO), got.at[1])
    project(HALO)

    def gf_make(lo, count):
        gfp[lo : lo + count, :] = (
            mm(g[lo : lo + count, 0:256], kw[:, 0:256], 1, 1)
            + mm(g[lo : lo + count, 256:512], vw[:, 0:256], 1, 1)
            + mm(g[lo : lo + count, 512:768], kw[:, 256:512], 1, 1)
            + mm(g[lo : lo + count, 768:1024], vw[:, 256:512], 1, 1)
        ).astype(BF16)

    def gf_cross(i):
        sends.start(
            rows_at(gfp, 128 * i + 64 * (1 - s), 64), gx.at[pl.ds(64 * i, 64)],
            gsem.at[1 + i], base + c, 1 - s,
        )

    def gf_add(i):
        await_bytes(gx.at[pl.ds(64 * i, 64)], gsem.at[1 + i])

        def add(t, _):
            there = pl.ds(pl.multiple_of(64 * i + 16 * t, 16), 16)
            here = pl.ds(pl.multiple_of(128 * i + 64 * s + 16 * t, 16), 16)
            gx[there] = (gx[there].astype(F32) + gfp[here].astype(F32)).astype(BF16)
            return 0

        lax.fori_loop(0, 4, add, 0)

    def gf_home(i):
        for r in range(4):
            t = (c + r) % 4
            d = 8 * (i - 1) + 4 * s + t
            sends.start(
                rows_at(gx, 64 * i + 16 * t, 16), rows_at(rgf, slot, 16), gsem.at[5],
                base + d, home, ((d == c) & (home == s)) if r == 0 else None,
            )

    scale = HEAD ** -0.5
    n = OWN // 2
    col = lax.broadcasted_iota(jnp.int32, (n, 2 * n), 1)
    back = lax.broadcasted_iota(jnp.int32, (n, 2 * n), 0) + HALO - col
    window = (back >= 0) & (back < 8 * WINDOW) & (back % 8 == 0)
    keep = (window & ((z > 0) | (col >= HALO)), window)

    first_tile = (1, 0)

    def attend(pair, tile):
        lo = tile * n
        two = range(2)
        cols = [slice(128 * h, 128 * h + 128) for h in two]
        vcols = [slice(256 + 128 * h, 384 + 128 * h) for h in two]
        heads = [slice(256 * pair + 128 * h, 256 * pair + 128 * h + 128) for h in two]
        q = [qc[pair, lo : lo + n, cols[h]] for h in two]
        cot = [qc[pair, lo : lo + n, vcols[h]] for h in two]
        k = [k_scr[lo : lo + 2 * n, heads[h]] for h in two]
        v = [v_scr[lo : lo + 2 * n, heads[h]] for h in two]
        scores = [jnp.where(keep[tile], mm(q[h], k[h], 1, 1) * scale, -jnp.inf) for h in two]
        dp = [mm(cot[h], v[h], 1, 1) for h in two]
        e = [jnp.exp(scores[h] - jnp.max(scores[h], axis=-1, keepdims=True)) for h in two]
        w = [e[h] / jnp.sum(e[h], axis=-1, keepdims=True) for h in two]
        rounded = [w[h].astype(BF16) for h in two]
        wd = [w[h] * dp[h] for h in two]
        spread = [jnp.sum(wd[h], axis=-1, keepdims=True) for h in two]
        ds = [(w[h] * (dp[h] - spread[h]) * scale).astype(BF16) for h in two]
        for h in two:
            ag[pair, lo : lo + n, cols[h]] = mm(rounded[h], v[h], 1, 0).astype(BF16)
            ag[pair, lo : lo + n, vcols[h]] = mm(ds[h], k[h], 1, 0).astype(BF16)
        for at, left, right in ((0, ds, q), (256, rounded, cot)):
            for h in two:
                to = slice(512 * pair + at + 128 * h, 512 * pair + at + 128 * h + 128)
                grad = mm(left[h], right[h], 0, 0)
                if tile == first_tile[pair]:
                    acc[lo : lo + 2 * n, to] = grad
                elif tile == 0:
                    acc[0:n, to] = grad[0:n]
                    acc[n : 2 * n, to] += grad[n:]
                else:
                    acc[n : 2 * n, to] += grad[0:n]
                    acc[2 * n :, to] = grad[n:]

    def ag_home(pair, tile):
        for r in range(8):
            d = 8 * tile + (c + r) % 8
            sends.start(
                rows_at(ag.at[pair], 16 * d, 16), rows_at(rag.at[s, pair], slot, 16), gsem.at[0],
                base + d, home, ((home == s) & (d == c)) if r == 0 else None,
            )

    def c_view(r, h):
        return wc.at[r % NZ, pl.ds(2 * h, 2)]

    def c_make(*steps):
        for r in steps:
            wc[r] = mm(rt[zi[r]].reshape(256, ALL), g[:, :CW], 1, 0).astype(BF16).reshape(
                4, 4, 16, CW
            )

    def c_step(chains, k):
        for way, h, length, first in chains:
            own = c_view(way * (length - k), h)
            src = own
            if k > 0:
                src = cb.at[first + k - 1]
                await_bytes(src, csem.at[first + k - 1])

                def add(i, _):
                    src[i] = (src[i].astype(F32) + own[i].astype(F32)).astype(BF16)
                    return 0

                lax.fori_loop(0, 2, add, 0)
            sends.start(src, cb.at[first + k], csem.at[first + k], nxt if way == 1 else prv, s)

    def ab_make(out, r, lhs, lo, count):
        v = mm(lhs.reshape(512, ALL), g[:, lo : lo + 128 * count], 1, 0).astype(BF16)
        for t in range(count):
            out[t, r] = v[:, 128 * t : 128 * t + 128].reshape(8, 4, 16, 128)

    up_x, down_x = (base + y * 4 + xi[1], s), (base + y * 4 + xi[3], s)
    up_y, down_y = (base + yi[1] * 4 + x, s), (base + yi[3] * 4 + x, s)
    plane_rings, line_rings = [], []
    for t in range(NT):
        part, q = (0, t) if t < NA else (1, t - NA)
        own = (wa, wb)[part].at[q]
        mid = plane_out.at[t]
        over = (yi, xi)[part]
        plane_rings.append(Ring4(
            sends, lambda r, h, own=own: own.at[r, pl.ds(4 * h, 4)],
            *((up_x, down_x), (up_y, down_y))[part],
            (ring_up.at[t], ring_down.at[t], ring_below.at[t], ring_above.at[t]),
            r1sem.at[t], mid,
        ))
        line_rings.append(Line4(
            sends, mid.at[:, over[0]], [mid.at[:, over[r]] for r in range(1, 4)],
            [((base + yi[r] * 4 + x, base + y * 4 + xi[r])[part], s) for r in range(1, 4)],
            ring2.at[t], r2sem.at[t], z_out.at[t],
        ))

    def a_make(r):
        ab_make(wa, r, rt[:, :, xi[r]], CW, NA)

    def b_make(r):
        ab_make(wb, r, rt[:, yi[r]], CW + 128 * NA, NB)

    def ring_start():
        a_make(2)
        for t in range(NA):
            plane_rings[t].first()
        b_make(2)
        for t in range(NA, NT):
            plane_rings[t].first()
        a_make(1)
        a_make(3)
        for t in range(NA):
            plane_rings[t].direct()
        b_make(1)
        b_make(3)
        for t in range(NA, NT):
            plane_rings[t].direct()

    def c_first():
        c_make(4)
        c_step(CHAINS[:2], 0)

    def c_second():
        c_make(3, 5)
        c_step(CHAINS[2:], 0)

    def gf_own():
        gf_make(HALO, OWN)
        gf_cross(1)
        gf_cross(2)

    def gf_home1():
        gf_add(1)
        gf_home(1)

    def gf_home2():
        gf_add(2)
        await_bytes(gh, gsem.at[4])

        def add_halo(t, _):
            there = pl.ds(pl.multiple_of(128 + 16 * t, 16), 16)
            here = pl.ds(pl.multiple_of(16 * t, 16), 16)
            gx[there] = (gx[there].astype(F32) + gh[here].astype(F32)).astype(BF16)
            return 0

        lax.fori_loop(0, 4, add_halo, 0)
        gf_home(2)

    def own_slices():
        c_make(1, 7, 0)
        a_make(0)
        b_make(0)

    def to_line(t):
        plane_rings[t].third()
        line_rings[t].start()

    def unpack(value):
        v = value.astype(F32)
        return (
            jnp.concatenate([v[0:8], v[16:24]], axis=0).astype(BF16),
            jnp.concatenate([v[8:16], v[24:32]], axis=0).astype(BF16),
        )

    leaving = [
        pltpu.make_async_copy(src, dst, osem.at[i])
        for i, (src, dst) in enumerate((
            (att_out, att_hbm), (gq_out, gq_hbm), (gf_out, gf_hbm), (gk_out, gk_hbm),
            (gv_out, gv_hbm),
        ))
    ]

    def att_unpack():
        await_bytes(rag, gsem.at[0])
        for core in range(2):
            for pair in range(2):
                to = HALF * core + 256 * pair
                for out, at in ((att_out, 0), (gq_out, 256)):
                    for t in range(4):
                        part = rag[core, pair, 32 * t : 32 * t + 32, at : at + 256]
                        for fr, v in enumerate(unpack(part)):
                            out[fr, 16 * t : 16 * t + 16, to : to + 256] = v
        leaving[0].start()
        leaving[1].start()

    def gf_unpack():
        await_bytes(rgf, gsem.at[5])
        for t in range(4):
            for fr, v in enumerate(unpack(rgf[32 * t : 32 * t + 32, :])):
                gf_out[fr, 16 * t : 16 * t + 16, :] = v
        leaving[2].start()

    def z_sends():
        for r in range(1, NZ):
            sends.start(z_out.at[:, zi[r]], z_in.at[r - 1], endsem.at[0], zi[r] * PLANE + c, s)

    def c_last():
        for way, h, length, first in CHAINS:
            await_bytes(cb.at[first + length - 1], csem.at[first + length - 1])
        for h, (p, m) in enumerate(((3, 13), (10, 7))):
            own = c_view(0, h)

            def add(i, _):
                rc[2 * h + i] = (
                    own[i].astype(F32) + cb[p, i].astype(F32) + cb[m, i].astype(F32)
                ).astype(BF16)
                return 0

            lax.fori_loop(0, 2, add, 0)
        for r in range(1, PLANE):
            yy, xx = yi[r // 4], xi[r % 4]
            sends.start(rc.at[yy, xx], cc.at[r - 1], endsem.at[1], base + yy * 4 + xx, s)

    def halo_relay():
        for r in range(4):
            i = 4 * s + xi[r]
            block = rows_at(rows, 16 * i, 16)
            await_bytes(block, hsem.at[i])
            sends.start(block, block, got.at[2], base + c, 1 - s)

    def first_heads(tile):
        if tile == 1:
            await_bytes(qc.at[0], qsem.at[0])
        else:
            halo_relay()
            await_bytes(other(0), got.at[2])
            project(0)
        attend(0, tile)
        if tile == 0:
            g[:, :512] = acc[:, :512].astype(BF16)

    def second_heads(tile):
        if tile == 0:
            await_bytes(qc.at[1], qsem.at[1])
        attend(1, tile)
        if tile == 1:
            g[HALO:, 512:] = acc[HALO:, 512:].astype(BF16)

    def gf_halo():
        g[:HALO, 512:] = acc[:HALO, 512:].astype(BF16)
        gf_make(0, HALO)
        gf_cross(0)

    def gf_back():
        gf_add(0)
        sends.start(gx.at[pl.ds(0, 64)], gh, gsem.at[4], prv, s)

    steps = {
        "p01": lambda: first_heads(1), "p00": lambda: first_heads(0),
        "p10": lambda: second_heads(0), "p11": lambda: second_heads(1),
        "a01": lambda: ag_home(0, 1), "a00": lambda: ag_home(0, 0),
        "a11": lambda: ag_home(1, 1), "a10": lambda: ag_home(1, 0),
        "gfH": gf_halo, "gf0": gf_back,
        "T0": c_first, "B0": c_second, "F": ring_start, "gf": gf_own, "home1": gf_home1,
        "home2": gf_home2, "c26": lambda: c_make(2, 6), "c170": own_slices,
        "att": att_unpack, "gfout": gf_unpack, "Z": z_sends, "C": c_last,
    }
    for k in range(1, 4):
        steps["T%d" % k] = lambda k=k: c_step(CHAINS[:2], k)
        steps["B%d" % k] = lambda k=k: c_step(CHAINS[2:], k)
    for t in range(NT):
        steps["S%d" % t] = plane_rings[t].second
        steps["H%d" % t] = lambda t=t: to_line(t)
        steps["M%d" % t] = line_rings[t].finish
    for name in ORDER:
        steps[name]()

    def gathered(buf, own, count):
        return lax.fori_loop(0, count, lambda i, v: v + buf[i].astype(F32), own.astype(F32))

    await_bytes(z_in, endsem.at[0])
    for t in range(NT):
        out, at = (gk_out, 256 + 128 * t) if t < NA else (gv_out, 256 + 128 * (t - NA))
        out[:, at : at + 128] = gathered(z_in.at[:, t], z_out[t, z], NZ - 1)
    await_bytes(cc, endsem.at[1])
    last = gathered(cc, rc[y, x], PLANE - 1)
    gk_out[:, 0:256] = last[:, 0:256]
    gv_out[:, 0:256] = last[:, 256:512]
    leaving[3].start()
    leaving[4].start()
    sends.finish()
    for copy in leaving:
        copy.wait()


def leave_kernel(*refs):
    into, out = (
        [pltpu.make_async_copy(src[i], dst[i], sem.at[i]) for i in range(5)]
        for src, dst, sem in ((refs[0:5], refs[10:15], refs[15]), (refs[10:15], refs[5:10], refs[16]))
    )
    for copy in into:
        copy.start()
    for i in range(5):
        into[i].wait()
        out[i].start()
    for copy in out:
        copy.wait()


def shards(features, queries, cotangent, key_weight, value_weight):
    def vm(*shape, dtype=BF16):
        return pltpu.VMEM(shape, dtype)

    sem = pltpu.SemaphoreType.DMA
    t = NT
    scratch = [
        vm(2, 64, 1024), vm(2, 64, D), vm(2, 64, 1024), vm(16, HALF, dtype=F32),
        vm(16, HALF, dtype=F32),
        vm(2, 64, D), vm(2, 64, 2 * HALF), vm(2, 64, 2 * HALF),
        vm(D, HALF), vm(D, HALF), vm(128, D), vm(2, 2, 128, HALF),
        vm(ALL, D), vm(2, OWN, HALF), vm(8, 4, 4, 16, ALL),
        vm(ALL, HALF), vm(ALL, HALF), vm(ALL, 2 * HALF, dtype=F32), vm(ALL, 2 * HALF),
        vm(2, OWN, HALF), vm(ALL, D), vm(2, 2, 128, HALF), vm(128, D),
        vm(192, D), vm(64, D),
        vm(NA, 4, 8, 4, 16, 128), vm(NB, 4, 8, 4, 16, 128), vm(8, 4, 4, 16, CW),
        vm(t, 4, 4, 16, 128), vm(t, 4, 4, 16, 128), vm(t, 8, 4, 16, 128), vm(t, 8, 4, 16, 128),
        vm(t, 8, 4, 16, 128),
        vm(t, 3, 8, 16, 128),
        vm(t, 8, 16, 128), vm(NZ - 1, t, 16, 128),
        vm(14, 2, 4, 16, CW), vm(4, 4, 16, CW), vm(PLANE - 1, 16, CW),
        sem((200,)), sem((9,)), sem((3,)), sem((2,)), sem((16,)), sem((8,)), sem((6,)),
        sem((t, 6)), sem((t,)), sem((14,)), sem((2,)), sem((5,)),
    ]
    vmem = pl.BlockSpec(memory_space=pltpu.VMEM)
    hbm = pl.BlockSpec(memory_space=pl.ANY)
    results = pl.pallas_call(
        kernel,
        out_shape=(
            jax.ShapeDtypeStruct(queries.shape, BF16),
            jax.ShapeDtypeStruct(features.shape, BF16),
            jax.ShapeDtypeStruct(queries.shape, BF16),
            jax.ShapeDtypeStruct((16, HALF), F32),
            jax.ShapeDtypeStruct((16, HALF), F32),
        ),
        in_specs=[hbm] * 5,
        out_specs=[hbm] * 5,
        scratch_shapes=scratch,
        compiler_params=pltpu.CompilerParams(
            collective_id=0, has_side_effects=True, vmem_limit_bytes=61 * MIB
        ),
    )(features, queries, cotangent, key_weight, value_weight)
    return pl.pallas_call(
        leave_kernel,
        out_shape=tuple(jax.ShapeDtypeStruct(v.shape, v.dtype) for v in results),
        in_specs=[hbm] * 5,
        out_specs=[hbm] * 5,
        scratch_shapes=[pltpu.VMEM(v.shape, v.dtype) for v in results] + [sem((5,)), sem((5,))],
        compiler_params=pltpu.CompilerParams(vmem_limit_bytes=61 * MIB),
    )(*results)


def solution(mesh):
    rows = P("tm", "space", None)
    return jax.shard_map(
        shards,
        mesh=mesh,
        in_specs=(rows, rows, rows, P(None, "space"), P(None, "space")),
        out_specs=(rows, rows, rows, P("tm", "space"), P("tm", "space")),
        check_vma=False,
    )
```

```python
import jax
import jax.numpy as jnp
from jax import lax
from jax.experimental import pallas as pl
from jax.experimental.pallas import tpu as pltpu
from jax.sharding import PartitionSpec as P

HEAD = 128
WINDOW = 16
PLANE = 16
NZ = 8
OWN = 256
HALO = 128
ALL = HALO + OWN
HALF = 512
D = 2048
F32 = jnp.float32
BF16 = jnp.bfloat16
MIB = 2**20


def mm(a, b, ca, cb):
    return lax.dot_general(a, b, (((ca,), (cb,)), ((), ())), preferred_element_type=F32)


def rows_at(ref, start, count):
    return ref.at[pl.ds(pl.multiple_of(start, 16), count)]


def signal(sem, tm, core):
    pl.semaphore_signal(
        sem, inc=1, device_id=(tm, core), device_id_type=pl.DeviceIdType.MESH
    )


def await_bytes(ref, sem):
    pltpu.make_async_copy(ref, ref, sem).wait()


class Sends:
    def __init__(self, sems):
        self.sems, self.used, self.waits = sems, 0, []

    def start(self, src, dst, rsem, tm, core, self_if=None):
        copy = pltpu.make_async_remote_copy(
            src_ref=src, dst_ref=dst, send_sem=self.sems.at[self.used], recv_sem=rsem,
            device_id=(tm, core), device_id_type=pl.DeviceIdType.MESH,
        )
        self.used += 1
        if self_if is None:
            copy.start()
        else:
            pl.when(self_if)(lambda: pltpu.make_async_copy(src, dst, rsem).start())
            pl.when(jnp.logical_not(self_if))(copy.start)
        self.waits.append((copy, self_if))

    def settle(self, i):
        if self.waits[i] is None:
            return
        copy, self_if = self.waits[i]
        self.waits[i] = None
        if self_if is None:
            copy.wait_send()
        else:
            pl.when(jnp.logical_not(self_if))(copy.wait_send)

    def finish(self):
        for i in range(self.used):
            self.settle(i)


class Ring4:
    def __init__(self, sends, view, up, down, bufs, sems, out):
        self.sends, self.view, self.up, self.down = sends, view, up, down
        self.bufs, self.sems, self.out = bufs, sems, out

    def first(self):
        self.sends.start(self.view(2, 0), self.bufs[0], self.sems.at[0], *self.up)
        self.sends.start(self.view(2, 1), self.bufs[1], self.sems.at[1], *self.down)

    def direct(self):
        _, _, below, above = self.bufs
        h = below.shape[0] // 2
        self.sends.start(self.view(1, 1), below.at[pl.ds(h, h)], self.sems.at[2], *self.up)
        self.sends.start(self.view(3, 0), above.at[pl.ds(0, h)], self.sems.at[3], *self.down)

    def second(self):
        from_below, from_above, below, above = self.bufs
        h = below.shape[0] // 2
        for buf, sem, view, dst, dsem, dev in (
            (from_below, 0, self.view(1, 0), below.at[pl.ds(0, h)], 4, self.up),
            (from_above, 1, self.view(3, 1), above.at[pl.ds(h, h)], 5, self.down),
        ):
            await_bytes(buf, self.sems.at[sem])

            def add(i, _):
                buf[i] = (buf[i].astype(F32) + view[i].astype(F32)).astype(BF16)
                return 0

            lax.fori_loop(0, h, add, 0)
            self.sends.start(buf, dst, self.sems.at[dsem], *dev)

    def third(self):
        _, _, below, above = self.bufs
        h = below.shape[0] // 2
        await_bytes(below.at[pl.ds(h, h)], self.sems.at[2])
        await_bytes(above.at[pl.ds(0, h)], self.sems.at[3])
        await_bytes(below.at[pl.ds(0, h)], self.sems.at[4])
        await_bytes(above.at[pl.ds(h, h)], self.sems.at[5])
        for half in range(2):
            own = self.view(0, half)

            def add(i, _):
                j = half * h + i
                self.out[j] = (
                    own[i].astype(F32) + below[j].astype(F32) + above[j].astype(F32)
                ).astype(BF16)
                return 0

            lax.fori_loop(0, h, add, 0)


NA, NB = 2, 2
NT = NA + NB
CW = 1024 - 128 * NT
ORDER = (
    "p01", "a01", "p00", "T0", "B0", "a00", "p10", "gfH", "p11", "F", "T1", "gf0", "gf", "c26",
    "B1", "S0", "S2", "S1", "S3", "c170", "T2", "H0", "H2", "H1", "H3", "a10", "a11", "home1",
    "home2", "B2", "T3", "M0", "M2", "M1", "M3", "Z", "C", "att", "gfout",
)
class Line4:
    def __init__(self, sends, mine, slices, devices, buf, sem, out):
        self.sends, self.mine, self.slices, self.devices = sends, mine, slices, devices
        self.buf, self.sem, self.out = buf, sem, out

    def start(self):
        for r, (piece, device) in enumerate(zip(self.slices, self.devices)):
            self.sends.start(piece, self.buf.at[r], self.sem, *device)

    def finish(self):
        await_bytes(self.buf, self.sem)

        def add(i, _):
            total = self.mine[i].astype(F32)
            for r in range(3):
                total += self.buf[r, i].astype(F32)
            self.out[i] = total.astype(BF16)
            return 0

        lax.fori_loop(0, NZ, add, 0)


CHAINS = ((1, 0, 4, 0), (-1, 1, 4, 4), (1, 1, 3, 8), (-1, 0, 3, 11))


def kernel(
    f_hbm, q_hbm, c_hbm, kw_hbm, vw_hbm,
    att_hbm, gf_hbm, gq_hbm, gk_hbm, gv_hbm,
    att_out, gf_out, gq_out, gk_out, gv_out,
    f_ref, q_ref, c_ref, kw, vw, fb, qcb, rows, qc, rt, k_scr, v_scr, acc, g, ag, gfp, rag, rgf, gx, gh,
    wa, wb, wc, ring_up, ring_down, ring_below, ring_above, plane_out,
    ring2, z_out, z_in, cb, rc, cc,
    send, wsem, got, qsem, fsem, hsem, gsem, r1sem, r2sem, csem, endsem, osem,
):
    tm = lax.axis_index("tm")
    s = lax.axis_index("space")
    z, c = tm // PLANE, tm % PLANE
    y, x = c // 4, c % 4
    base = z * PLANE
    zi = [(z + r) % NZ for r in range(NZ)]
    yi = [(y + r) % 4 for r in range(4)]
    xi = [(x + r) % 4 for r in range(4)]
    nxt, prv = zi[1] * PLANE + c, zi[7] * PLANE + c

    loads = [
        pltpu.make_async_copy(src, dst, wsem.at[i])
        for i, (src, dst) in enumerate(
            ((q_hbm, q_ref), (c_hbm, c_ref), (kw_hbm, kw), (vw_hbm, vw))
        )
    ]
    f_loads = [
        pltpu.make_async_copy(
            f_hbm.at[:, 16 * t : 16 * t + 16], f_ref.at[:, 16 * t : 16 * t + 16], wsem.at[5 + t]
        )
        for t in range(4)
    ]
    for copy in f_loads:
        copy.start()
    barrier = pltpu.get_barrier_semaphore()
    for r in range(1, PLANE):
        for core in range(2):
            signal(barrier, base + (c + r) % PLANE, core)
    signal(barrier, base + c, 1 - s)
    for r in range(1, NZ):
        signal(barrier, zi[r] * PLANE + c, s)

    def pack(ref, out, cols, at, waits=None):
        w = cols[1] - cols[0]
        for t in range(4):
            if waits:
                waits[t].wait()
            p, q = (ref[i, 16 * t : 16 * t + 16, cols[0] : cols[1]].astype(F32) for i in range(2))
            out[32 * t : 32 * t + 32, at : at + w] = jnp.concatenate(
                [p[:8], q[:8], p[8:], q[8:]], axis=0
            ).astype(BF16)

    for copy in loads:
        copy.start()
    pack(f_ref, fb, (0, D), 0, f_loads)
    pl.semaphore_wait(barrier, 2 * (PLANE - 1) + 1 + NZ - 1)

    sends = Sends(send)
    home = c % 2
    slot = 16 * (c // 2)
    to = (c // 4) % 2
    mine = c % 2 == s
    for r in range(8):
        j = (c // 2 + r) % 8
        sends.start(
            rows_at(fb, 16 * j, 16), rows_at(rows, HALO + 16 * c, 16), fsem.at[c],
            base + 2 * j + s, to, (mine & (to == s)) if r == 0 else None,
        )
    loads[0].wait()
    loads[1].wait()
    for pair in range(2):
        for core in range(2):
            at = HALF * core + 256 * pair
            pack(q_ref, qcb.at[core, pair], (at, at + 256), 0)
            pack(c_ref, qcb.at[core, pair], (at, at + 256), 256)
    for pair in range(2):
        for r in range(8):
            j = (c // 2 + r) % 8
            if pair == 0:
                sends.settle(r)
            for o in range(2):
                core = (s + o) % 2
                sends.start(
                    rows_at(qcb.at[core, pair], 16 * j, 16), rows_at(qc.at[pair], 16 * c, 16),
                    qsem.at[pair], base + 2 * j + s, core, mine if r == 0 and o == 0 else None,
                )
    for r in range(4):
        i = 4 * s + xi[r]
        block = rows_at(rows, HALO + 128 + 16 * i, 16)
        await_bytes(block, fsem.at[8 + i])
        sends.start(block, rows_at(rows, 16 * i, 16), hsem.at[i], nxt, s)
        sends.start(block, block, got.at[0], base + c, 1 - s)
    for r in range(4):
        i = 4 * s + xi[r]
        block = rows_at(rows, HALO + 16 * i, 16)
        await_bytes(block, fsem.at[i])
        sends.start(block, block, got.at[1], base + c, 1 - s)

    def project(lo):
        part = rows[lo : lo + 128, :]
        k_scr[lo : lo + 128, :] = mm(part, kw[...], 1, 0).astype(BF16)
        v_scr[lo : lo + 128, :] = mm(part, vw[...], 1, 0).astype(BF16)
        rt[:, :, :, :, lo : lo + 128] = part.T.reshape(8, 4, 4, 16, 128)

    def other(lo):
        return rows_at(rows, lo + 64 * (1 - s), 64)

    loads[2].wait()
    loads[3].wait()
    await_bytes(other(HALO + 128), got.at[0])
    project(HALO + 128)
    await_bytes(other(HALO), got.at[1])
    project(HALO)

    def gf_make(lo, count):
        gfp[lo : lo + count, :] = (
            mm(g[lo : lo + count, 0:256], kw[:, 0:256], 1, 1)
            + mm(g[lo : lo + count, 256:512], vw[:, 0:256], 1, 1)
            + mm(g[lo : lo + count, 512:768], kw[:, 256:512], 1, 1)
            + mm(g[lo : lo + count, 768:1024], vw[:, 256:512], 1, 1)
        ).astype(BF16)

    def gf_cross(i):
        sends.start(
            rows_at(gfp, 128 * i + 64 * (1 - s), 64), gx.at[pl.ds(64 * i, 64)],
            gsem.at[1 + i], base + c, 1 - s,
        )

    def gf_add(i):
        await_bytes(gx.at[pl.ds(64 * i, 64)], gsem.at[1 + i])

        def add(t, _):
            there = pl.ds(pl.multiple_of(64 * i + 16 * t, 16), 16)
            here = pl.ds(pl.multiple_of(128 * i + 64 * s + 16 * t, 16), 16)
            gx[there] = (gx[there].astype(F32) + gfp[here].astype(F32)).astype(BF16)
            return 0

        lax.fori_loop(0, 4, add, 0)

    def gf_home(i):
        for r in range(4):
            t = (c + r) % 4
            d = 8 * (i - 1) + 4 * s + t
            sends.start(
                rows_at(gx, 64 * i + 16 * t, 16), rows_at(rgf, slot, 16), gsem.at[5],
                base + d, home, ((d == c) & (home == s)) if r == 0 else None,
            )

    scale = HEAD ** -0.5
    n = OWN // 2
    col = lax.broadcasted_iota(jnp.int32, (n, 2 * n), 1)
    back = lax.broadcasted_iota(jnp.int32, (n, 2 * n), 0) + HALO - col
    window = (back >= 0) & (back < 8 * WINDOW) & (back % 8 == 0)
    keep = (window & ((z > 0) | (col >= HALO)), window)

    first_tile = (1, 0)

    def attend(pair, tile):
        lo = tile * n
        two = range(2)
        cols = [slice(128 * h, 128 * h + 128) for h in two]
        vcols = [slice(256 + 128 * h, 384 + 128 * h) for h in two]
        heads = [slice(256 * pair + 128 * h, 256 * pair + 128 * h + 128) for h in two]
        q = [qc[pair, lo : lo + n, cols[h]] for h in two]
        cot = [qc[pair, lo : lo + n, vcols[h]] for h in two]
        k = [k_scr[lo : lo + 2 * n, heads[h]] for h in two]
        v = [v_scr[lo : lo + 2 * n, heads[h]] for h in two]
        scores = [jnp.where(keep[tile], mm(q[h], k[h], 1, 1) * scale, -jnp.inf) for h in two]
        dp = [mm(cot[h], v[h], 1, 1) for h in two]
        e = [jnp.exp(scores[h] - jnp.max(scores[h], axis=-1, keepdims=True)) for h in two]
        w = [e[h] / jnp.sum(e[h], axis=-1, keepdims=True) for h in two]
        rounded = [w[h].astype(BF16) for h in two]
        wd = [w[h] * dp[h] for h in two]
        spread = [jnp.sum(wd[h], axis=-1, keepdims=True) for h in two]
        ds = [(w[h] * (dp[h] - spread[h]) * scale).astype(BF16) for h in two]
        for h in two:
            ag[pair, lo : lo + n, cols[h]] = mm(rounded[h], v[h], 1, 0).astype(BF16)
            ag[pair, lo : lo + n, vcols[h]] = mm(ds[h], k[h], 1, 0).astype(BF16)
        for at, left, right in ((0, ds, q), (256, rounded, cot)):
            for h in two:
                to = slice(512 * pair + at + 128 * h, 512 * pair + at + 128 * h + 128)
                grad = mm(left[h], right[h], 0, 0)
                if tile == first_tile[pair]:
                    acc[lo : lo + 2 * n, to] = grad
                elif tile == 0:
                    acc[0:n, to] = grad[0:n]
                    acc[n : 2 * n, to] += grad[n:]
                else:
                    acc[n : 2 * n, to] += grad[0:n]
                    acc[2 * n :, to] = grad[n:]

    def ag_home(pair, tile):
        for r in range(8):
            d = 8 * tile + (c + r) % 8
            sends.start(
                rows_at(ag.at[pair], 16 * d, 16), rows_at(rag.at[s, pair], slot, 16), gsem.at[0],
                base + d, home, ((home == s) & (d == c)) if r == 0 else None,
            )

    def c_view(r, h):
        return wc.at[r % NZ, pl.ds(2 * h, 2)]

    def c_make(*steps):
        for r in steps:
            wc[r] = mm(rt[zi[r]].reshape(256, ALL), g[:, :CW], 1, 0).astype(BF16).reshape(
                4, 4, 16, CW
            )

    def c_step(chains, k):
        for way, h, length, first in chains:
            own = c_view(way * (length - k), h)
            src = own
            if k > 0:
                src = cb.at[first + k - 1]
                await_bytes(src, csem.at[first + k - 1])

                def add(i, _):
                    src[i] = (src[i].astype(F32) + own[i].astype(F32)).astype(BF16)
                    return 0

                lax.fori_loop(0, 2, add, 0)
            sends.start(src, cb.at[first + k], csem.at[first + k], nxt if way == 1 else prv, s)

    def ab_make(out, r, lhs, lo, count):
        v = mm(lhs.reshape(512, ALL), g[:, lo : lo + 128 * count], 1, 0).astype(BF16)
        for t in range(count):
            out[t, r] = v[:, 128 * t : 128 * t + 128].reshape(8, 4, 16, 128)

    up_x, down_x = (base + y * 4 + xi[1], s), (base + y * 4 + xi[3], s)
    up_y, down_y = (base + yi[1] * 4 + x, s), (base + yi[3] * 4 + x, s)
    plane_rings, line_rings = [], []
    for t in range(NT):
        part, q = (0, t) if t < NA else (1, t - NA)
        own = (wa, wb)[part].at[q]
        mid = plane_out.at[t]
        over = (yi, xi)[part]
        plane_rings.append(Ring4(
            sends, lambda r, h, own=own: own.at[r, pl.ds(4 * h, 4)],
            *((up_x, down_x), (up_y, down_y))[part],
            (ring_up.at[t], ring_down.at[t], ring_below.at[t], ring_above.at[t]),
            r1sem.at[t], mid,
        ))
        line_rings.append(Line4(
            sends, mid.at[:, over[0]], [mid.at[:, over[r]] for r in range(1, 4)],
            [((base + yi[r] * 4 + x, base + y * 4 + xi[r])[part], s) for r in range(1, 4)],
            ring2.at[t], r2sem.at[t], z_out.at[t],
        ))

    def a_make(r):
        ab_make(wa, r, rt[:, :, xi[r]], CW, NA)

    def b_make(r):
        ab_make(wb, r, rt[:, yi[r]], CW + 128 * NA, NB)

    def ring_start():
        a_make(2)
        for t in range(NA):
            plane_rings[t].first()
        b_make(2)
        for t in range(NA, NT):
            plane_rings[t].first()
        a_make(1)
        a_make(3)
        for t in range(NA):
            plane_rings[t].direct()
        b_make(1)
        b_make(3)
        for t in range(NA, NT):
            plane_rings[t].direct()

    def c_first():
        c_make(4)
        c_step(CHAINS[:2], 0)

    def c_second():
        c_make(3, 5)
        c_step(CHAINS[2:], 0)

    def gf_own():
        gf_make(HALO, OWN)
        gf_cross(1)
        gf_cross(2)

    def gf_home1():
        gf_add(1)
        gf_home(1)

    def gf_home2():
        gf_add(2)
        await_bytes(gh, gsem.at[4])

        def add_halo(t, _):
            there = pl.ds(pl.multiple_of(128 + 16 * t, 16), 16)
            here = pl.ds(pl.multiple_of(16 * t, 16), 16)
            gx[there] = (gx[there].astype(F32) + gh[here].astype(F32)).astype(BF16)
            return 0

        lax.fori_loop(0, 4, add_halo, 0)
        gf_home(2)

    def own_slices():
        c_make(1, 7, 0)
        a_make(0)
        b_make(0)

    def to_line(t):
        plane_rings[t].third()
        line_rings[t].start()

    def unpack(value):
        v = value.astype(F32)
        return (
            jnp.concatenate([v[0:8], v[16:24]], axis=0).astype(BF16),
            jnp.concatenate([v[8:16], v[24:32]], axis=0).astype(BF16),
        )

    leaving = [
        pltpu.make_async_copy(src, dst, osem.at[i])
        for i, (src, dst) in enumerate((
            (att_out, att_hbm), (gq_out, gq_hbm), (gf_out, gf_hbm), (gk_out, gk_hbm),
            (gv_out, gv_hbm),
        ))
    ]

    def att_unpack():
        await_bytes(rag, gsem.at[0])
        for core in range(2):
            for pair in range(2):
                to = HALF * core + 256 * pair
                for out, at in ((att_out, 0), (gq_out, 256)):
                    for t in range(4):
                        part = rag[core, pair, 32 * t : 32 * t + 32, at : at + 256]
                        for fr, v in enumerate(unpack(part)):
                            out[fr, 16 * t : 16 * t + 16, to : to + 256] = v
        leaving[0].start()
        leaving[1].start()

    def gf_unpack():
        await_bytes(rgf, gsem.at[5])
        for t in range(4):
            for fr, v in enumerate(unpack(rgf[32 * t : 32 * t + 32, :])):
                gf_out[fr, 16 * t : 16 * t + 16, :] = v
        leaving[2].start()

    def z_sends():
        for r in range(1, NZ):
            sends.start(z_out.at[:, zi[r]], z_in.at[r - 1], endsem.at[0], zi[r] * PLANE + c, s)

    def c_last():
        for way, h, length, first in CHAINS:
            await_bytes(cb.at[first + length - 1], csem.at[first + length - 1])
        for h, (p, m) in enumerate(((3, 13), (10, 7))):
            own = c_view(0, h)

            def add(i, _):
                rc[2 * h + i] = (
                    own[i].astype(F32) + cb[p, i].astype(F32) + cb[m, i].astype(F32)
                ).astype(BF16)
                return 0

            lax.fori_loop(0, 2, add, 0)
        for r in range(1, PLANE):
            yy, xx = yi[r // 4], xi[r % 4]
            sends.start(rc.at[yy, xx], cc.at[r - 1], endsem.at[1], base + yy * 4 + xx, s)

    def halo_relay():
        for r in range(4):
            i = 4 * s + xi[r]
            block = rows_at(rows, 16 * i, 16)
            await_bytes(block, hsem.at[i])
            sends.start(block, block, got.at[2], base + c, 1 - s)

    def first_heads(tile):
        if tile == 1:
            await_bytes(qc.at[0], qsem.at[0])
        else:
            halo_relay()
            await_bytes(other(0), got.at[2])
            project(0)
        attend(0, tile)
        if tile == 0:
            g[:, :512] = acc[:, :512].astype(BF16)

    def second_heads(tile):
        if tile == 0:
            await_bytes(qc.at[1], qsem.at[1])
        attend(1, tile)
        if tile == 1:
            g[HALO:, 512:] = acc[HALO:, 512:].astype(BF16)

    def gf_halo():
        g[:HALO, 512:] = acc[:HALO, 512:].astype(BF16)
        gf_make(0, HALO)
        gf_cross(0)

    def gf_back():
        gf_add(0)
        sends.start(gx.at[pl.ds(0, 64)], gh, gsem.at[4], prv, s)

    steps = {
        "p01": lambda: first_heads(1), "p00": lambda: first_heads(0),
        "p10": lambda: second_heads(0), "p11": lambda: second_heads(1),
        "a01": lambda: ag_home(0, 1), "a00": lambda: ag_home(0, 0),
        "a11": lambda: ag_home(1, 1), "a10": lambda: ag_home(1, 0),
        "gfH": gf_halo, "gf0": gf_back,
        "T0": c_first, "B0": c_second, "F": ring_start, "gf": gf_own, "home1": gf_home1,
        "home2": gf_home2, "c26": lambda: c_make(2, 6), "c170": own_slices,
        "att": att_unpack, "gfout": gf_unpack, "Z": z_sends, "C": c_last,
    }
    for k in range(1, 4):
        steps["T%d" % k] = lambda k=k: c_step(CHAINS[:2], k)
        steps["B%d" % k] = lambda k=k: c_step(CHAINS[2:], k)
    for t in range(NT):
        steps["S%d" % t] = plane_rings[t].second
        steps["H%d" % t] = lambda t=t: to_line(t)
        steps["M%d" % t] = line_rings[t].finish
    for name in ORDER:
        steps[name]()

    def gathered(buf, own, count):
        return lax.fori_loop(0, count, lambda i, v: v + buf[i].astype(F32), own.astype(F32))

    await_bytes(z_in, endsem.at[0])
    for t in range(NT):
        out, at = (gk_out, 256 + 128 * t) if t < NA else (gv_out, 256 + 128 * (t - NA))
        out[:, at : at + 128] = gathered(z_in.at[:, t], z_out[t, z], NZ - 1)
    await_bytes(cc, endsem.at[1])
    last = gathered(cc, rc[y, x], PLANE - 1)
    gk_out[:, 0:256] = last[:, 0:256]
    gv_out[:, 0:256] = last[:, 256:512]
    leaving[3].start()
    leaving[4].start()
    sends.finish()
    for copy in leaving:
        copy.wait()


def leave_kernel(*refs):
    into, out = (
        [pltpu.make_async_copy(src[i], dst[i], sem.at[i]) for i in range(5)]
        for src, dst, sem in ((refs[0:5], refs[10:15], refs[15]), (refs[10:15], refs[5:10], refs[16]))
    )
    for copy in into:
        copy.start()
    for i in range(5):
        into[i].wait()
        out[i].start()
    for copy in out:
        copy.wait()


def shards(features, queries, cotangent, key_weight, value_weight):
    def vm(*shape, dtype=BF16):
        return pltpu.VMEM(shape, dtype)

    sem = pltpu.SemaphoreType.DMA
    t = NT
    scratch = [
        vm(2, 64, 1024), vm(2, 64, D), vm(2, 64, 1024), vm(16, HALF, dtype=F32),
        vm(16, HALF, dtype=F32),
        vm(2, 64, D), vm(2, 64, 2 * HALF), vm(2, 64, 2 * HALF),
        vm(D, HALF), vm(D, HALF), vm(128, D), vm(2, 2, 128, HALF),
        vm(ALL, D), vm(2, OWN, HALF), vm(8, 4, 4, 16, ALL),
        vm(ALL, HALF), vm(ALL, HALF), vm(ALL, 2 * HALF, dtype=F32), vm(ALL, 2 * HALF),
        vm(2, OWN, HALF), vm(ALL, D), vm(2, 2, 128, HALF), vm(128, D),
        vm(192, D), vm(64, D),
        vm(NA, 4, 8, 4, 16, 128), vm(NB, 4, 8, 4, 16, 128), vm(8, 4, 4, 16, CW),
        vm(t, 4, 4, 16, 128), vm(t, 4, 4, 16, 128), vm(t, 8, 4, 16, 128), vm(t, 8, 4, 16, 128),
        vm(t, 8, 4, 16, 128),
        vm(t, 3, 8, 16, 128),
        vm(t, 8, 16, 128), vm(NZ - 1, t, 16, 128),
        vm(14, 2, 4, 16, CW), vm(4, 4, 16, CW), vm(PLANE - 1, 16, CW),
        sem((200,)), sem((9,)), sem((3,)), sem((2,)), sem((16,)), sem((8,)), sem((6,)),
        sem((t, 6)), sem((t,)), sem((14,)), sem((2,)), sem((5,)),
    ]
    vmem = pl.BlockSpec(memory_space=pltpu.VMEM)
    hbm = pl.BlockSpec(memory_space=pl.ANY)
    results = pl.pallas_call(
        kernel,
        out_shape=(
            jax.ShapeDtypeStruct(queries.shape, BF16),
            jax.ShapeDtypeStruct(features.shape, BF16),
            jax.ShapeDtypeStruct(queries.shape, BF16),
            jax.ShapeDtypeStruct((16, HALF), F32),
            jax.ShapeDtypeStruct((16, HALF), F32),
        ),
        in_specs=[hbm] * 5,
        out_specs=[hbm] * 5,
        scratch_shapes=scratch,
        compiler_params=pltpu.CompilerParams(
            collective_id=0, has_side_effects=True, vmem_limit_bytes=61 * MIB
        ),
    )(features, queries, cotangent, key_weight, value_weight)
    return pl.pallas_call(
        leave_kernel,
        out_shape=tuple(jax.ShapeDtypeStruct(v.shape, v.dtype) for v in results),
        in_specs=[hbm] * 5,
        out_specs=[hbm] * 5,
        scratch_shapes=[pltpu.VMEM(v.shape, v.dtype) for v in results] + [sem((5,)), sem((5,))],
        compiler_params=pltpu.CompilerParams(vmem_limit_bytes=61 * MIB),
    )(*results)


def solution(mesh):
    rows = P("tm", "space", None)
    return jax.shard_map(
        shards,
        mesh=mesh,
        in_specs=(rows, rows, rows, P(None, "space"), P(None, "space")),
        out_specs=(rows, rows, rows, P("tm", "space"), P("tm", "space")),
        check_vma=False,
    )
```

```python
import jax
import jax.numpy as jnp
from jax import lax
from jax.experimental import pallas as pl
from jax.experimental.pallas import tpu as pltpu
from jax.sharding import PartitionSpec as P

HEAD = 128
WINDOW = 16
PLANE = 16
NZ = 8
OWN = 256
HALO = 128
ALL = HALO + OWN
HALF = 512
D = 2048
F32 = jnp.float32
BF16 = jnp.bfloat16
MIB = 2**20


def mm(a, b, ca, cb):
    return lax.dot_general(a, b, (((ca,), (cb,)), ((), ())), preferred_element_type=F32)


def rows_at(ref, start, count):
    return ref.at[pl.ds(pl.multiple_of(start, 16), count)]


def signal(sem, tm, core):
    pl.semaphore_signal(
        sem, inc=1, device_id=(tm, core), device_id_type=pl.DeviceIdType.MESH
    )


def await_bytes(ref, sem):
    pltpu.make_async_copy(ref, ref, sem).wait()


class Sends:
    def __init__(self, sems):
        self.sems, self.used, self.waits = sems, 0, []

    def start(self, src, dst, rsem, tm, core, self_if=None):
        copy = pltpu.make_async_remote_copy(
            src_ref=src, dst_ref=dst, send_sem=self.sems.at[self.used], recv_sem=rsem,
            device_id=(tm, core), device_id_type=pl.DeviceIdType.MESH,
        )
        self.used += 1
        if self_if is None:
            copy.start()
        else:
            pl.when(self_if)(lambda: pltpu.make_async_copy(src, dst, rsem).start())
            pl.when(jnp.logical_not(self_if))(copy.start)
        self.waits.append((copy, self_if))

    def settle(self, i):
        if self.waits[i] is None:
            return
        copy, self_if = self.waits[i]
        self.waits[i] = None
        if self_if is None:
            copy.wait_send()
        else:
            pl.when(jnp.logical_not(self_if))(copy.wait_send)

    def finish(self):
        for i in range(self.used):
            self.settle(i)


class Ring4:
    def __init__(self, sends, view, up, down, bufs, sems, out):
        self.sends, self.view, self.up, self.down = sends, view, up, down
        self.bufs, self.sems, self.out = bufs, sems, out

    def first(self):
        self.sends.start(self.view(2, 0), self.bufs[0], self.sems.at[0], *self.up)
        self.sends.start(self.view(2, 1), self.bufs[1], self.sems.at[1], *self.down)

    def direct(self):
        _, _, below, above = self.bufs
        h = below.shape[0] // 2
        self.sends.start(self.view(1, 1), below.at[pl.ds(h, h)], self.sems.at[2], *self.up)
        self.sends.start(self.view(3, 0), above.at[pl.ds(0, h)], self.sems.at[3], *self.down)

    def second(self):
        from_below, from_above, below, above = self.bufs
        h = below.shape[0] // 2
        for buf, sem, view, dst, dsem, dev in (
            (from_below, 0, self.view(1, 0), below.at[pl.ds(0, h)], 4, self.up),
            (from_above, 1, self.view(3, 1), above.at[pl.ds(h, h)], 5, self.down),
        ):
            await_bytes(buf, self.sems.at[sem])

            def add(i, _):
                buf[i] = (buf[i].astype(F32) + view[i].astype(F32)).astype(BF16)
                return 0

            lax.fori_loop(0, h, add, 0)
            self.sends.start(buf, dst, self.sems.at[dsem], *dev)

    def third(self):
        _, _, below, above = self.bufs
        h = below.shape[0] // 2
        await_bytes(below.at[pl.ds(h, h)], self.sems.at[2])
        await_bytes(above.at[pl.ds(0, h)], self.sems.at[3])
        await_bytes(below.at[pl.ds(0, h)], self.sems.at[4])
        await_bytes(above.at[pl.ds(h, h)], self.sems.at[5])
        for half in range(2):
            own = self.view(0, half)

            def add(i, _):
                j = half * h + i
                self.out[j] = (
                    own[i].astype(F32) + below[j].astype(F32) + above[j].astype(F32)
                ).astype(BF16)
                return 0

            lax.fori_loop(0, h, add, 0)


NA, NB = 2, 2
NT = NA + NB
CW = 1024 - 128 * NT
ORDER = (
    "p01", "a01", "p00", "T0", "B0", "a00", "p10", "gfH", "p11", "F", "T1", "gf0", "c26", "B1",
    "gf", "S0", "S2", "S1", "S3", "T2", "c170", "H0", "H2", "H1", "H3", "home1", "home2", "a10",
    "a11", "B2", "T3", "M0", "M2", "M1", "M3", "Z", "C", "att", "gfout",
)
class Line4:
    def __init__(self, sends, mine, slices, devices, buf, sem, out):
        self.sends, self.mine, self.slices, self.devices = sends, mine, slices, devices
        self.buf, self.sem, self.out = buf, sem, out

    def start(self):
        for r, (piece, device) in enumerate(zip(self.slices, self.devices)):
            self.sends.start(piece, self.buf.at[r], self.sem, *device)

    def finish(self):
        await_bytes(self.buf, self.sem)

        def add(i, _):
            total = self.mine[i].astype(F32)
            for r in range(3):
                total += self.buf[r, i].astype(F32)
            self.out[i] = total.astype(BF16)
            return 0

        lax.fori_loop(0, NZ, add, 0)


CHAINS = ((1, 0, 4, 0), (-1, 1, 4, 4), (1, 1, 3, 8), (-1, 0, 3, 11))


def kernel(
    f_hbm, q_hbm, c_hbm, kw_hbm, vw_hbm,
    att_hbm, gf_hbm, gq_hbm, gk_hbm, gv_hbm,
    att_out, gf_out, gq_out, gk_out, gv_out,
    f_ref, q_ref, c_ref, kw, vw, fb, qcb, rows, qc, rt, k_scr, v_scr, acc, g, ag, gfp, rag, rgf, gx, gh,
    wa, wb, wc, ring_up, ring_down, ring_below, ring_above, plane_out,
    ring2, z_out, z_in, cb, rc, cc,
    send, wsem, got, qsem, fsem, hsem, gsem, r1sem, r2sem, csem, endsem, osem,
):
    tm = lax.axis_index("tm")
    s = lax.axis_index("space")
    z, c = tm // PLANE, tm % PLANE
    y, x = c // 4, c % 4
    base = z * PLANE
    zi = [(z + r) % NZ for r in range(NZ)]
    yi = [(y + r) % 4 for r in range(4)]
    xi = [(x + r) % 4 for r in range(4)]
    nxt, prv = zi[1] * PLANE + c, zi[7] * PLANE + c

    loads = [
        pltpu.make_async_copy(src, dst, wsem.at[i])
        for i, (src, dst) in enumerate(
            ((q_hbm, q_ref), (c_hbm, c_ref), (kw_hbm, kw), (vw_hbm, vw))
        )
    ]
    f_loads = [
        pltpu.make_async_copy(
            f_hbm.at[:, 16 * t : 16 * t + 16], f_ref.at[:, 16 * t : 16 * t + 16], wsem.at[5 + t]
        )
        for t in range(4)
    ]
    for copy in f_loads:
        copy.start()
    barrier = pltpu.get_barrier_semaphore()
    for r in range(1, PLANE):
        for core in range(2):
            signal(barrier, base + (c + r) % PLANE, core)
    signal(barrier, base + c, 1 - s)
    for r in range(1, NZ):
        signal(barrier, zi[r] * PLANE + c, s)

    def pack(ref, out, cols, at, waits=None):
        w = cols[1] - cols[0]
        for t in range(4):
            if waits:
                waits[t].wait()
            p, q = (ref[i, 16 * t : 16 * t + 16, cols[0] : cols[1]].astype(F32) for i in range(2))
            out[32 * t : 32 * t + 32, at : at + w] = jnp.concatenate(
                [p[:8], q[:8], p[8:], q[8:]], axis=0
            ).astype(BF16)

    for copy in loads:
        copy.start()
    pack(f_ref, fb, (0, D), 0, f_loads)
    pl.semaphore_wait(barrier, 2 * (PLANE - 1) + 1 + NZ - 1)

    sends = Sends(send)
    home = c % 2
    slot = 16 * (c // 2)
    to = (c // 4) % 2
    mine = c % 2 == s
    for r in range(8):
        j = (c // 2 + r) % 8
        sends.start(
            rows_at(fb, 16 * j, 16), rows_at(rows, HALO + 16 * c, 16), fsem.at[c],
            base + 2 * j + s, to, (mine & (to == s)) if r == 0 else None,
        )
    loads[0].wait()
    loads[1].wait()
    for pair in range(2):
        for core in range(2):
            at = HALF * core + 256 * pair
            pack(q_ref, qcb.at[core, pair], (at, at + 256), 0)
            pack(c_ref, qcb.at[core, pair], (at, at + 256), 256)
    for pair in range(2):
        for r in range(8):
            j = (c // 2 + r) % 8
            if pair == 0:
                sends.settle(r)
            for o in range(2):
                core = (s + o) % 2
                sends.start(
                    rows_at(qcb.at[core, pair], 16 * j, 16), rows_at(qc.at[pair], 16 * c, 16),
                    qsem.at[pair], base + 2 * j + s, core, mine if r == 0 and o == 0 else None,
                )
    for r in range(4):
        i = 4 * s + xi[r]
        block = rows_at(rows, HALO + 128 + 16 * i, 16)
        await_bytes(block, fsem.at[8 + i])
        sends.start(block, rows_at(rows, 16 * i, 16), hsem.at[i], nxt, s)
        sends.start(block, block, got.at[0], base + c, 1 - s)
    for r in range(4):
        i = 4 * s + xi[r]
        block = rows_at(rows, HALO + 16 * i, 16)
        await_bytes(block, fsem.at[i])
        sends.start(block, block, got.at[1], base + c, 1 - s)

    def project(lo, pairs=(0, 1)):
        part = rows[lo : lo + 128, :]
        for pair in pairs:
            heads = slice(256 * pair, 256 * pair + 256)
            k_scr[lo : lo + 128, heads] = mm(part, kw[:, heads], 1, 0).astype(BF16)
            v_scr[lo : lo + 128, heads] = mm(part, vw[:, heads], 1, 0).astype(BF16)
        if 0 in pairs:
            rt[:, :, :, :, lo : lo + 128] = part.T.reshape(8, 4, 4, 16, 128)

    def other(lo):
        return rows_at(rows, lo + 64 * (1 - s), 64)

    loads[2].wait()
    loads[3].wait()
    await_bytes(other(HALO + 128), got.at[0])
    project(HALO + 128)
    await_bytes(other(HALO), got.at[1])
    project(HALO)

    def gf_make(lo, count):
        gfp[lo : lo + count, :] = (
            mm(g[lo : lo + count, 0:256], kw[:, 0:256], 1, 1)
            + mm(g[lo : lo + count, 256:512], vw[:, 0:256], 1, 1)
            + mm(g[lo : lo + count, 512:768], kw[:, 256:512], 1, 1)
            + mm(g[lo : lo + count, 768:1024], vw[:, 256:512], 1, 1)
        ).astype(BF16)

    def gf_cross(i):
        sends.start(
            rows_at(gfp, 128 * i + 64 * (1 - s), 64), gx.at[pl.ds(64 * i, 64)],
            gsem.at[1 + i], base + c, 1 - s,
        )

    def gf_add(i):
        await_bytes(gx.at[pl.ds(64 * i, 64)], gsem.at[1 + i])

        def add(t, _):
            there = pl.ds(pl.multiple_of(64 * i + 16 * t, 16), 16)
            here = pl.ds(pl.multiple_of(128 * i + 64 * s + 16 * t, 16), 16)
            gx[there] = (gx[there].astype(F32) + gfp[here].astype(F32)).astype(BF16)
            return 0

        lax.fori_loop(0, 4, add, 0)

    def gf_home(i):
        for r in range(4):
            t = (c + r) % 4
            d = 8 * (i - 1) + 4 * s + t
            sends.start(
                rows_at(gx, 64 * i + 16 * t, 16), rows_at(rgf, slot, 16), gsem.at[5],
                base + d, home, ((d == c) & (home == s)) if r == 0 else None,
            )

    scale = HEAD ** -0.5
    n = OWN // 2
    col = lax.broadcasted_iota(jnp.int32, (n, 2 * n), 1)
    back = lax.broadcasted_iota(jnp.int32, (n, 2 * n), 0) + HALO - col
    window = (back >= 0) & (back < 8 * WINDOW) & (back % 8 == 0)
    keep = (window & ((z > 0) | (col >= HALO)), window)

    first_tile = (1, 0)

    def attend(pair, tile):
        lo = tile * n
        two = range(2)
        cols = [slice(128 * h, 128 * h + 128) for h in two]
        vcols = [slice(256 + 128 * h, 384 + 128 * h) for h in two]
        heads = [slice(256 * pair + 128 * h, 256 * pair + 128 * h + 128) for h in two]
        q = [qc[pair, lo : lo + n, cols[h]] for h in two]
        cot = [qc[pair, lo : lo + n, vcols[h]] for h in two]
        k = [k_scr[lo : lo + 2 * n, heads[h]] for h in two]
        v = [v_scr[lo : lo + 2 * n, heads[h]] for h in two]
        scores = [jnp.where(keep[tile], mm(q[h], k[h], 1, 1) * scale, -jnp.inf) for h in two]
        dp = [mm(cot[h], v[h], 1, 1) for h in two]
        e = [jnp.exp(scores[h] - jnp.max(scores[h], axis=-1, keepdims=True)) for h in two]
        w = [e[h] / jnp.sum(e[h], axis=-1, keepdims=True) for h in two]
        rounded = [w[h].astype(BF16) for h in two]
        wd = [w[h] * dp[h] for h in two]
        spread = [jnp.sum(wd[h], axis=-1, keepdims=True) for h in two]
        ds = [(w[h] * (dp[h] - spread[h]) * scale).astype(BF16) for h in two]
        for h in two:
            ag[pair, lo : lo + n, cols[h]] = mm(rounded[h], v[h], 1, 0).astype(BF16)
            ag[pair, lo : lo + n, vcols[h]] = mm(ds[h], k[h], 1, 0).astype(BF16)
        for at, left, right in ((0, ds, q), (256, rounded, cot)):
            for h in two:
                to = slice(512 * pair + at + 128 * h, 512 * pair + at + 128 * h + 128)
                grad = mm(left[h], right[h], 0, 0)
                if tile == first_tile[pair]:
                    acc[lo : lo + 2 * n, to] = grad
                elif tile == 0:
                    acc[0:n, to] = grad[0:n]
                    acc[n : 2 * n, to] += grad[n:]
                else:
                    acc[n : 2 * n, to] += grad[0:n]
                    acc[2 * n :, to] = grad[n:]

    def ag_home(pair, tile):
        for r in range(8):
            d = 8 * tile + (c + r) % 8
            sends.start(
                rows_at(ag.at[pair], 16 * d, 16), rows_at(rag.at[s, pair], slot, 16), gsem.at[0],
                base + d, home, ((home == s) & (d == c)) if r == 0 else None,
            )

    def c_view(r, h):
        return wc.at[r % NZ, pl.ds(2 * h, 2)]

    def c_make(*steps):
        for r in steps:
            wc[r] = mm(rt[zi[r]].reshape(256, ALL), g[:, :CW], 1, 0).astype(BF16).reshape(
                4, 4, 16, CW
            )

    def c_step(chains, k):
        for way, h, length, first in chains:
            own = c_view(way * (length - k), h)
            src = own
            if k > 0:
                src = cb.at[first + k - 1]
                await_bytes(src, csem.at[first + k - 1])

                def add(i, _):
                    src[i] = (src[i].astype(F32) + own[i].astype(F32)).astype(BF16)
                    return 0

                lax.fori_loop(0, 2, add, 0)
            sends.start(src, cb.at[first + k], csem.at[first + k], nxt if way == 1 else prv, s)

    def ab_make(out, r, lhs, lo, count):
        v = mm(lhs.reshape(512, ALL), g[:, lo : lo + 128 * count], 1, 0).astype(BF16)
        for t in range(count):
            out[t, r] = v[:, 128 * t : 128 * t + 128].reshape(8, 4, 16, 128)

    up_x, down_x = (base + y * 4 + xi[1], s), (base + y * 4 + xi[3], s)
    up_y, down_y = (base + yi[1] * 4 + x, s), (base + yi[3] * 4 + x, s)
    plane_rings, line_rings = [], []
    for t in range(NT):
        part, q = (0, t) if t < NA else (1, t - NA)
        own = (wa, wb)[part].at[q]
        mid = plane_out.at[t]
        over = (yi, xi)[part]
        plane_rings.append(Ring4(
            sends, lambda r, h, own=own: own.at[r, pl.ds(4 * h, 4)],
            *((up_x, down_x), (up_y, down_y))[part],
            (ring_up.at[t], ring_down.at[t], ring_below.at[t], ring_above.at[t]),
            r1sem.at[t], mid,
        ))
        line_rings.append(Line4(
            sends, mid.at[:, over[0]], [mid.at[:, over[r]] for r in range(1, 4)],
            [((base + yi[r] * 4 + x, base + y * 4 + xi[r])[part], s) for r in range(1, 4)],
            ring2.at[t], r2sem.at[t], z_out.at[t],
        ))

    def a_make(r):
        ab_make(wa, r, rt[:, :, xi[r]], CW, NA)

    def b_make(r):
        ab_make(wb, r, rt[:, yi[r]], CW + 128 * NA, NB)

    def ring_start():
        a_make(2)
        for t in range(NA):
            plane_rings[t].first()
        b_make(2)
        for t in range(NA, NT):
            plane_rings[t].first()
        a_make(1)
        a_make(3)
        for t in range(NA):
            plane_rings[t].direct()
        b_make(1)
        b_make(3)
        for t in range(NA, NT):
            plane_rings[t].direct()

    def c_first():
        c_make(4)
        c_step(CHAINS[:2], 0)

    def c_second():
        c_make(3, 5)
        c_step(CHAINS[2:], 0)

    def gf_own():
        gf_make(HALO, OWN)
        gf_cross(1)
        gf_cross(2)

    def gf_home1():
        gf_add(1)
        gf_home(1)

    def gf_home2():
        gf_add(2)
        await_bytes(gh, gsem.at[4])

        def add_halo(t, _):
            there = pl.ds(pl.multiple_of(128 + 16 * t, 16), 16)
            here = pl.ds(pl.multiple_of(16 * t, 16), 16)
            gx[there] = (gx[there].astype(F32) + gh[here].astype(F32)).astype(BF16)
            return 0

        lax.fori_loop(0, 4, add_halo, 0)
        gf_home(2)

    def own_slices():
        c_make(1, 7, 0)
        a_make(0)
        b_make(0)

    def to_line(t):
        plane_rings[t].third()
        line_rings[t].start()

    def unpack(value):
        v = value.astype(F32)
        return (
            jnp.concatenate([v[0:8], v[16:24]], axis=0).astype(BF16),
            jnp.concatenate([v[8:16], v[24:32]], axis=0).astype(BF16),
        )

    leaving = [
        pltpu.make_async_copy(src, dst, osem.at[i])
        for i, (src, dst) in enumerate((
            (att_out, att_hbm), (gq_out, gq_hbm), (gf_out, gf_hbm), (gk_out, gk_hbm),
            (gv_out, gv_hbm),
        ))
    ]

    def att_unpack():
        await_bytes(rag, gsem.at[0])
        for core in range(2):
            for pair in range(2):
                to = HALF * core + 256 * pair
                for out, at in ((att_out, 0), (gq_out, 256)):
                    for t in range(4):
                        part = rag[core, pair, 32 * t : 32 * t + 32, at : at + 256]
                        for fr, v in enumerate(unpack(part)):
                            out[fr, 16 * t : 16 * t + 16, to : to + 256] = v
        leaving[0].start()
        leaving[1].start()

    def gf_unpack():
        await_bytes(rgf, gsem.at[5])
        for t in range(4):
            for fr, v in enumerate(unpack(rgf[32 * t : 32 * t + 32, :])):
                gf_out[fr, 16 * t : 16 * t + 16, :] = v
        leaving[2].start()

    def z_sends():
        for r in range(1, NZ):
            sends.start(z_out.at[:, zi[r]], z_in.at[r - 1], endsem.at[0], zi[r] * PLANE + c, s)

    def c_last():
        for way, h, length, first in CHAINS:
            await_bytes(cb.at[first + length - 1], csem.at[first + length - 1])
        for h, (p, m) in enumerate(((3, 13), (10, 7))):
            own = c_view(0, h)

            def add(i, _):
                rc[2 * h + i] = (
                    own[i].astype(F32) + cb[p, i].astype(F32) + cb[m, i].astype(F32)
                ).astype(BF16)
                return 0

            lax.fori_loop(0, 2, add, 0)
        for r in range(1, PLANE):
            yy, xx = yi[r // 4], xi[r % 4]
            sends.start(rc.at[yy, xx], cc.at[r - 1], endsem.at[1], base + yy * 4 + xx, s)

    def halo_relay():
        for r in range(4):
            i = 4 * s + xi[r]
            block = rows_at(rows, 16 * i, 16)
            await_bytes(block, hsem.at[i])
            sends.start(block, block, got.at[2], base + c, 1 - s)

    def first_heads(tile):
        if tile == 1:
            await_bytes(qc.at[0], qsem.at[0])
        else:
            halo_relay()
            await_bytes(other(0), got.at[2])
            project(0, (0,))
        attend(0, tile)
        if tile == 0:
            g[:, :512] = acc[:, :512].astype(BF16)

    def second_heads(tile):
        if tile == 0:
            project(0, (1,))
            await_bytes(qc.at[1], qsem.at[1])
        attend(1, tile)
        if tile == 1:
            g[HALO:, 512:] = acc[HALO:, 512:].astype(BF16)

    def gf_halo():
        g[:HALO, 512:] = acc[:HALO, 512:].astype(BF16)
        gf_make(0, HALO)
        gf_cross(0)

    def gf_back():
        gf_add(0)
        sends.start(gx.at[pl.ds(0, 64)], gh, gsem.at[4], prv, s)

    steps = {
        "p01": lambda: first_heads(1), "p00": lambda: first_heads(0),
        "p10": lambda: second_heads(0), "p11": lambda: second_heads(1),
        "a01": lambda: ag_home(0, 1), "a00": lambda: ag_home(0, 0),
        "a11": lambda: ag_home(1, 1), "a10": lambda: ag_home(1, 0),
        "gfH": gf_halo, "gf0": gf_back,
        "T0": c_first, "B0": c_second, "F": ring_start, "gf": gf_own, "home1": gf_home1,
        "home2": gf_home2, "c26": lambda: c_make(2, 6), "c170": own_slices,
        "att": att_unpack, "gfout": gf_unpack, "Z": z_sends, "C": c_last,
    }
    for k in range(1, 4):
        steps["T%d" % k] = lambda k=k: c_step(CHAINS[:2], k)
        steps["B%d" % k] = lambda k=k: c_step(CHAINS[2:], k)
    for t in range(NT):
        steps["S%d" % t] = plane_rings[t].second
        steps["H%d" % t] = lambda t=t: to_line(t)
        steps["M%d" % t] = line_rings[t].finish
    for name in ORDER:
        steps[name]()

    def gathered(buf, own, count):
        return lax.fori_loop(0, count, lambda i, v: v + buf[i].astype(F32), own.astype(F32))

    await_bytes(z_in, endsem.at[0])
    for t in range(NT):
        out, at = (gk_out, 256 + 128 * t) if t < NA else (gv_out, 256 + 128 * (t - NA))
        out[:, at : at + 128] = gathered(z_in.at[:, t], z_out[t, z], NZ - 1)
    await_bytes(cc, endsem.at[1])
    last = gathered(cc, rc[y, x], PLANE - 1)
    gk_out[:, 0:256] = last[:, 0:256]
    gv_out[:, 0:256] = last[:, 256:512]
    leaving[3].start()
    leaving[4].start()
    sends.finish()
    for copy in leaving:
        copy.wait()


def leave_kernel(*refs):
    into, out = (
        [pltpu.make_async_copy(src[i], dst[i], sem.at[i]) for i in range(5)]
        for src, dst, sem in ((refs[0:5], refs[10:15], refs[15]), (refs[10:15], refs[5:10], refs[16]))
    )
    for copy in into:
        copy.start()
    for i in range(5):
        into[i].wait()
        out[i].start()
    for copy in out:
        copy.wait()


def shards(features, queries, cotangent, key_weight, value_weight):
    def vm(*shape, dtype=BF16):
        return pltpu.VMEM(shape, dtype)

    sem = pltpu.SemaphoreType.DMA
    t = NT
    scratch = [
        vm(2, 64, 1024), vm(2, 64, D), vm(2, 64, 1024), vm(16, HALF, dtype=F32),
        vm(16, HALF, dtype=F32),
        vm(2, 64, D), vm(2, 64, 2 * HALF), vm(2, 64, 2 * HALF),
        vm(D, HALF), vm(D, HALF), vm(128, D), vm(2, 2, 128, HALF),
        vm(ALL, D), vm(2, OWN, HALF), vm(8, 4, 4, 16, ALL),
        vm(ALL, HALF), vm(ALL, HALF), vm(ALL, 2 * HALF, dtype=F32), vm(ALL, 2 * HALF),
        vm(2, OWN, HALF), vm(ALL, D), vm(2, 2, 128, HALF), vm(128, D),
        vm(192, D), vm(64, D),
        vm(NA, 4, 8, 4, 16, 128), vm(NB, 4, 8, 4, 16, 128), vm(8, 4, 4, 16, CW),
        vm(t, 4, 4, 16, 128), vm(t, 4, 4, 16, 128), vm(t, 8, 4, 16, 128), vm(t, 8, 4, 16, 128),
        vm(t, 8, 4, 16, 128),
        vm(t, 3, 8, 16, 128),
        vm(t, 8, 16, 128), vm(NZ - 1, t, 16, 128),
        vm(14, 2, 4, 16, CW), vm(4, 4, 16, CW), vm(PLANE - 1, 16, CW),
        sem((200,)), sem((9,)), sem((3,)), sem((2,)), sem((16,)), sem((8,)), sem((6,)),
        sem((t, 6)), sem((t,)), sem((14,)), sem((2,)), sem((5,)),
    ]
    vmem = pl.BlockSpec(memory_space=pltpu.VMEM)
    hbm = pl.BlockSpec(memory_space=pl.ANY)
    results = pl.pallas_call(
        kernel,
        out_shape=(
            jax.ShapeDtypeStruct(queries.shape, BF16),
            jax.ShapeDtypeStruct(features.shape, BF16),
            jax.ShapeDtypeStruct(queries.shape, BF16),
            jax.ShapeDtypeStruct((16, HALF), F32),
            jax.ShapeDtypeStruct((16, HALF), F32),
        ),
        in_specs=[hbm] * 5,
        out_specs=[hbm] * 5,
        scratch_shapes=scratch,
        compiler_params=pltpu.CompilerParams(
            collective_id=0, has_side_effects=True, vmem_limit_bytes=61 * MIB
        ),
    )(features, queries, cotangent, key_weight, value_weight)
    return pl.pallas_call(
        leave_kernel,
        out_shape=tuple(jax.ShapeDtypeStruct(v.shape, v.dtype) for v in results),
        in_specs=[hbm] * 5,
        out_specs=[hbm] * 5,
        scratch_shapes=[pltpu.VMEM(v.shape, v.dtype) for v in results] + [sem((5,)), sem((5,))],
        compiler_params=pltpu.CompilerParams(vmem_limit_bytes=61 * MIB),
    )(*results)


def solution(mesh):
    rows = P("tm", "space", None)
    return jax.shard_map(
        shards,
        mesh=mesh,
        in_specs=(rows, rows, rows, P(None, "space"), P(None, "space")),
        out_specs=(rows, rows, rows, P("tm", "space"), P("tm", "space")),
        check_vma=False,
    )
```

```python
import jax
import jax.numpy as jnp
from jax import lax
from jax.experimental import pallas as pl
from jax.experimental.pallas import tpu as pltpu
from jax.sharding import PartitionSpec as P

HEAD = 128
WINDOW = 16
PLANE = 16
NZ = 8
OWN = 256
HALO = 128
ALL = HALO + OWN
HALF = 512
D = 2048
F32 = jnp.float32
BF16 = jnp.bfloat16
MIB = 2**20


def mm(a, b, ca, cb):
    return lax.dot_general(a, b, (((ca,), (cb,)), ((), ())), preferred_element_type=F32)


def rows_at(ref, start, count):
    return ref.at[pl.ds(pl.multiple_of(start, 16), count)]


def signal(sem, tm, core):
    pl.semaphore_signal(
        sem, inc=1, device_id=(tm, core), device_id_type=pl.DeviceIdType.MESH
    )


def await_bytes(ref, sem):
    pltpu.make_async_copy(ref, ref, sem).wait()


class Sends:
    def __init__(self, sems):
        self.sems, self.used, self.waits = sems, 0, []

    def start(self, src, dst, rsem, tm, core, self_if=None):
        copy = pltpu.make_async_remote_copy(
            src_ref=src, dst_ref=dst, send_sem=self.sems.at[self.used], recv_sem=rsem,
            device_id=(tm, core), device_id_type=pl.DeviceIdType.MESH,
        )
        self.used += 1
        if self_if is None:
            copy.start()
        else:
            pl.when(self_if)(lambda: pltpu.make_async_copy(src, dst, rsem).start())
            pl.when(jnp.logical_not(self_if))(copy.start)
        self.waits.append((copy, self_if))

    def settle(self, i):
        if self.waits[i] is None:
            return
        copy, self_if = self.waits[i]
        self.waits[i] = None
        if self_if is None:
            copy.wait_send()
        else:
            pl.when(jnp.logical_not(self_if))(copy.wait_send)

    def finish(self):
        for i in range(self.used):
            self.settle(i)


class Ring4:
    def __init__(self, sends, view, up, down, bufs, sems, out):
        self.sends, self.view, self.up, self.down = sends, view, up, down
        self.bufs, self.sems, self.out = bufs, sems, out

    def first(self):
        self.sends.start(self.view(2, 0), self.bufs[0], self.sems.at[0], *self.up)
        self.sends.start(self.view(2, 1), self.bufs[1], self.sems.at[1], *self.down)

    def direct(self):
        _, _, below, above = self.bufs
        h = below.shape[0] // 2
        self.sends.start(self.view(1, 1), below.at[pl.ds(h, h)], self.sems.at[2], *self.up)
        self.sends.start(self.view(3, 0), above.at[pl.ds(0, h)], self.sems.at[3], *self.down)

    def second(self):
        from_below, from_above, below, above = self.bufs
        h = below.shape[0] // 2
        for buf, sem, view, dst, dsem, dev in (
            (from_below, 0, self.view(1, 0), below.at[pl.ds(0, h)], 4, self.up),
            (from_above, 1, self.view(3, 1), above.at[pl.ds(h, h)], 5, self.down),
        ):
            await_bytes(buf, self.sems.at[sem])

            def add(i, _):
                buf[i] = (buf[i].astype(F32) + view[i].astype(F32)).astype(BF16)
                return 0

            lax.fori_loop(0, h, add, 0)
            self.sends.start(buf, dst, self.sems.at[dsem], *dev)

    def third(self):
        _, _, below, above = self.bufs
        h = below.shape[0] // 2
        await_bytes(below.at[pl.ds(h, h)], self.sems.at[2])
        await_bytes(above.at[pl.ds(0, h)], self.sems.at[3])
        await_bytes(below.at[pl.ds(0, h)], self.sems.at[4])
        await_bytes(above.at[pl.ds(h, h)], self.sems.at[5])
        for half in range(2):
            own = self.view(0, half)

            def add(i, _):
                j = half * h + i
                self.out[j] = (
                    own[i].astype(F32) + below[j].astype(F32) + above[j].astype(F32)
                ).astype(BF16)
                return 0

            lax.fori_loop(0, h, add, 0)


NA, NB = 2, 2
NT = NA + NB
CW = 1024 - 128 * NT
ORDER = (
    "p01", "a01", "p00", "T0", "B0", "a00", "p10", "gfH", "p11", "F", "T1", "gf0", "gf", "c26",
    "B1", "S0", "S2", "S1", "S3", "T2", "c170", "H0", "H2", "H1", "H3", "a10", "a11", "home1",
    "home2", "B2", "T3", "M0", "M2", "M1", "M3", "Z", "C", "att", "gfout",
)
class Line4:
    def __init__(self, sends, mine, slices, devices, buf, sem, out):
        self.sends, self.mine, self.slices, self.devices = sends, mine, slices, devices
        self.buf, self.sem, self.out = buf, sem, out

    def start(self):
        for r, (piece, device) in enumerate(zip(self.slices, self.devices)):
            self.sends.start(piece, self.buf.at[r], self.sem, *device)

    def finish(self):
        await_bytes(self.buf, self.sem)

        def add(i, _):
            total = self.mine[i].astype(F32)
            for r in range(3):
                total += self.buf[r, i].astype(F32)
            self.out[i] = total.astype(BF16)
            return 0

        lax.fori_loop(0, NZ, add, 0)


CHAINS = ((1, 0, 4, 0), (-1, 1, 4, 4), (1, 1, 3, 8), (-1, 0, 3, 11))


def kernel(
    f_hbm, q_hbm, c_hbm, kw_hbm, vw_hbm,
    att_hbm, gf_hbm, gq_hbm, gk_hbm, gv_hbm,
    att_out, gf_out, gq_out, gk_out, gv_out,
    f_ref, q_ref, c_ref, kw, vw, fb, qcb, rows, qc, rt, k_scr, v_scr, acc, g, ag, gfp, rag, rgf, gx, gh,
    wa, wb, wc, ring_up, ring_down, ring_below, ring_above, plane_out,
    ring2, z_out, z_in, cb, rc, cc,
    send, wsem, got, qsem, fsem, hsem, gsem, r1sem, r2sem, csem, endsem, osem,
):
    tm = lax.axis_index("tm")
    s = lax.axis_index("space")
    z, c = tm // PLANE, tm % PLANE
    y, x = c // 4, c % 4
    base = z * PLANE
    zi = [(z + r) % NZ for r in range(NZ)]
    yi = [(y + r) % 4 for r in range(4)]
    xi = [(x + r) % 4 for r in range(4)]
    nxt, prv = zi[1] * PLANE + c, zi[7] * PLANE + c

    loads = [
        pltpu.make_async_copy(src, dst, wsem.at[i])
        for i, (src, dst) in enumerate(
            ((q_hbm, q_ref), (c_hbm, c_ref), (kw_hbm, kw), (vw_hbm, vw))
        )
    ]
    f_loads = [
        pltpu.make_async_copy(
            f_hbm.at[:, 16 * t : 16 * t + 16], f_ref.at[:, 16 * t : 16 * t + 16], wsem.at[5 + t]
        )
        for t in range(4)
    ]
    for copy in f_loads:
        copy.start()
    barrier = pltpu.get_barrier_semaphore()
    for r in range(1, PLANE):
        for core in range(2):
            signal(barrier, base + (c + r) % PLANE, core)
    signal(barrier, base + c, 1 - s)
    for r in range(1, NZ):
        signal(barrier, zi[r] * PLANE + c, s)

    def pack(ref, out, cols, at, waits=None):
        w = cols[1] - cols[0]
        for t in range(4):
            if waits:
                waits[t].wait()
            p, q = (ref[i, 16 * t : 16 * t + 16, cols[0] : cols[1]].astype(F32) for i in range(2))
            out[32 * t : 32 * t + 32, at : at + w] = jnp.concatenate(
                [p[:8], q[:8], p[8:], q[8:]], axis=0
            ).astype(BF16)

    for copy in loads:
        copy.start()
    pack(f_ref, fb, (0, D), 0, f_loads)
    pl.semaphore_wait(barrier, 2 * (PLANE - 1) + 1 + NZ - 1)

    sends = Sends(send)
    home = c % 2
    slot = 16 * (c // 2)
    to = (c // 4) % 2
    mine = c % 2 == s
    for r in range(8):
        j = (c // 2 + r) % 8
        sends.start(
            rows_at(fb, 16 * j, 16), rows_at(rows, HALO + 16 * c, 16), fsem.at[c],
            base + 2 * j + s, to, (mine & (to == s)) if r == 0 else None,
        )
    loads[0].wait()
    loads[1].wait()
    for pair in range(2):
        for core in range(2):
            at = HALF * core + 256 * pair
            pack(q_ref, qcb.at[core, pair], (at, at + 256), 0)
            pack(c_ref, qcb.at[core, pair], (at, at + 256), 256)
    for pair in range(2):
        for r in range(8):
            j = (c // 2 + r) % 8
            if pair == 0:
                sends.settle(r)
            for o in range(2):
                core = (s + o) % 2
                sends.start(
                    rows_at(qcb.at[core, pair], 16 * j, 16), rows_at(qc.at[pair], 16 * c, 16),
                    qsem.at[pair], base + 2 * j + s, core, mine if r == 0 and o == 0 else None,
                )
    for r in range(4):
        i = 4 * s + xi[r]
        block = rows_at(rows, HALO + 128 + 16 * i, 16)
        await_bytes(block, fsem.at[8 + i])
        sends.start(block, rows_at(rows, 16 * i, 16), hsem.at[i], nxt, s)
        sends.start(block, block, got.at[0], base + c, 1 - s)
    for r in range(4):
        i = 4 * s + xi[r]
        block = rows_at(rows, HALO + 16 * i, 16)
        await_bytes(block, fsem.at[i])
        sends.start(block, block, got.at[1], base + c, 1 - s)

    def project(lo):
        part = rows[lo : lo + 128, :]
        k_scr[lo : lo + 128, :] = mm(part, kw[...], 1, 0).astype(BF16)
        v_scr[lo : lo + 128, :] = mm(part, vw[...], 1, 0).astype(BF16)
        rt[:, :, :, :, lo : lo + 128] = part.T.reshape(8, 4, 4, 16, 128)

    def other(lo):
        return rows_at(rows, lo + 64 * (1 - s), 64)

    loads[2].wait()
    loads[3].wait()
    await_bytes(other(HALO + 128), got.at[0])
    project(HALO + 128)
    await_bytes(other(HALO), got.at[1])
    project(HALO)

    def gf_make(lo, count):
        gfp[lo : lo + count, :] = (
            mm(g[lo : lo + count, 0:256], kw[:, 0:256], 1, 1)
            + mm(g[lo : lo + count, 256:512], vw[:, 0:256], 1, 1)
            + mm(g[lo : lo + count, 512:768], kw[:, 256:512], 1, 1)
            + mm(g[lo : lo + count, 768:1024], vw[:, 256:512], 1, 1)
        ).astype(BF16)

    def gf_cross(i):
        sends.start(
            rows_at(gfp, 128 * i + 64 * (1 - s), 64), gx.at[pl.ds(64 * i, 64)],
            gsem.at[1 + i], base + c, 1 - s,
        )

    def gf_add(i):
        await_bytes(gx.at[pl.ds(64 * i, 64)], gsem.at[1 + i])

        def add(t, _):
            there = pl.ds(pl.multiple_of(64 * i + 16 * t, 16), 16)
            here = pl.ds(pl.multiple_of(128 * i + 64 * s + 16 * t, 16), 16)
            gx[there] = (gx[there].astype(F32) + gfp[here].astype(F32)).astype(BF16)
            return 0

        lax.fori_loop(0, 4, add, 0)

    def gf_home(i):
        for r in range(4):
            t = (c + r) % 4
            d = 8 * (i - 1) + 4 * s + t
            sends.start(
                rows_at(gx, 64 * i + 16 * t, 16), rows_at(rgf, slot, 16), gsem.at[5],
                base + d, home, ((d == c) & (home == s)) if r == 0 else None,
            )

    scale = HEAD ** -0.5
    n = OWN // 2
    col = lax.broadcasted_iota(jnp.int32, (n, 2 * n), 1)
    back = lax.broadcasted_iota(jnp.int32, (n, 2 * n), 0) + HALO - col
    window = (back >= 0) & (back < 8 * WINDOW) & (back % 8 == 0)
    keep = (window & ((z > 0) | (col >= HALO)), window)

    first_tile = (1, 0)

    def attend(pair, tile):
        lo = tile * n
        two = range(2)
        cols = [slice(128 * h, 128 * h + 128) for h in two]
        vcols = [slice(256 + 128 * h, 384 + 128 * h) for h in two]
        heads = [slice(256 * pair + 128 * h, 256 * pair + 128 * h + 128) for h in two]
        q = [qc[pair, lo : lo + n, cols[h]] for h in two]
        cot = [qc[pair, lo : lo + n, vcols[h]] for h in two]
        k = [k_scr[lo : lo + 2 * n, heads[h]] for h in two]
        v = [v_scr[lo : lo + 2 * n, heads[h]] for h in two]
        scores = [jnp.where(keep[tile], mm(q[h], k[h], 1, 1) * scale, -jnp.inf) for h in two]
        dp = [mm(cot[h], v[h], 1, 1) for h in two]
        e = [jnp.exp(scores[h] - jnp.max(scores[h], axis=-1, keepdims=True)) for h in two]
        w = [e[h] / jnp.sum(e[h], axis=-1, keepdims=True) for h in two]
        rounded = [w[h].astype(BF16) for h in two]
        wd = [w[h] * dp[h] for h in two]
        spread = [jnp.sum(wd[h], axis=-1, keepdims=True) for h in two]
        ds = [(w[h] * (dp[h] - spread[h]) * scale).astype(BF16) for h in two]
        for h in two:
            ag[pair, lo : lo + n, cols[h]] = mm(rounded[h], v[h], 1, 0).astype(BF16)
            ag[pair, lo : lo + n, vcols[h]] = mm(ds[h], k[h], 1, 0).astype(BF16)
        for at, left, right in ((0, ds, q), (256, rounded, cot)):
            for h in two:
                to = slice(512 * pair + at + 128 * h, 512 * pair + at + 128 * h + 128)
                grad = mm(left[h], right[h], 0, 0)
                if tile == first_tile[pair]:
                    acc[lo : lo + 2 * n, to] = grad
                elif tile == 0:
                    acc[0:n, to] = grad[0:n]
                    acc[n : 2 * n, to] += grad[n:]
                else:
                    acc[n : 2 * n, to] += grad[0:n]
                    acc[2 * n :, to] = grad[n:]

    def ag_home(pair, tile):
        for r in range(8):
            d = 8 * tile + (c + r) % 8
            sends.start(
                rows_at(ag.at[pair], 16 * d, 16), rows_at(rag.at[s, pair], slot, 16), gsem.at[0],
                base + d, home, ((home == s) & (d == c)) if r == 0 else None,
            )

    def c_view(r, h):
        return wc.at[r % NZ, pl.ds(2 * h, 2)]

    def c_make(*steps):
        for r in steps:
            wc[r] = mm(rt[zi[r]].reshape(256, ALL), g[:, :CW], 1, 0).astype(BF16).reshape(
                4, 4, 16, CW
            )

    def c_step(chains, k):
        for way, h, length, first in chains:
            own = c_view(way * (length - k), h)
            src = own
            if k > 0:
                src = cb.at[first + k - 1]
                await_bytes(src, csem.at[first + k - 1])

                def add(i, _):
                    src[i] = (src[i].astype(F32) + own[i].astype(F32)).astype(BF16)
                    return 0

                lax.fori_loop(0, 2, add, 0)
            sends.start(src, cb.at[first + k], csem.at[first + k], nxt if way == 1 else prv, s)

    def ab_make(out, r, lhs, lo, count):
        v = mm(lhs.reshape(512, ALL), g[:, lo : lo + 128 * count], 1, 0).astype(BF16)
        for t in range(count):
            out[t, r] = v[:, 128 * t : 128 * t + 128].reshape(8, 4, 16, 128)

    up_x, down_x = (base + y * 4 + xi[1], s), (base + y * 4 + xi[3], s)
    up_y, down_y = (base + yi[1] * 4 + x, s), (base + yi[3] * 4 + x, s)
    plane_rings, line_rings = [], []
    for t in range(NT):
        part, q = (0, t) if t < NA else (1, t - NA)
        own = (wa, wb)[part].at[q]
        mid = plane_out.at[t]
        over = (yi, xi)[part]
        plane_rings.append(Ring4(
            sends, lambda r, h, own=own: own.at[r, pl.ds(4 * h, 4)],
            *((up_x, down_x), (up_y, down_y))[part],
            (ring_up.at[t], ring_down.at[t], ring_below.at[t], ring_above.at[t]),
            r1sem.at[t], mid,
        ))
        line_rings.append(Line4(
            sends, mid.at[:, over[0]], [mid.at[:, over[r]] for r in range(1, 4)],
            [((base + yi[r] * 4 + x, base + y * 4 + xi[r])[part], s) for r in range(1, 4)],
            ring2.at[t], r2sem.at[t], z_out.at[t],
        ))

    def a_make(r):
        ab_make(wa, r, rt[:, :, xi[r]], CW, NA)

    def b_make(r):
        ab_make(wb, r, rt[:, yi[r]], CW + 128 * NA, NB)

    def ring_start():
        a_make(2)
        for t in range(NA):
            plane_rings[t].first()
        b_make(2)
        for t in range(NA, NT):
            plane_rings[t].first()
        a_make(1)
        a_make(3)
        for t in range(NA):
            plane_rings[t].direct()
        b_make(1)
        b_make(3)
        for t in range(NA, NT):
            plane_rings[t].direct()

    def c_first():
        c_make(4)
        c_step(CHAINS[:2], 0)

    def c_second():
        c_make(3, 5)
        c_step(CHAINS[2:], 0)

    def gf_own():
        gf_make(HALO, OWN)
        gf_cross(1)
        gf_cross(2)

    def gf_home1():
        gf_add(1)
        gf_home(1)

    def gf_home2():
        gf_add(2)
        await_bytes(gh, gsem.at[4])

        def add_halo(t, _):
            there = pl.ds(pl.multiple_of(128 + 16 * t, 16), 16)
            here = pl.ds(pl.multiple_of(16 * t, 16), 16)
            gx[there] = (gx[there].astype(F32) + gh[here].astype(F32)).astype(BF16)
            return 0

        lax.fori_loop(0, 4, add_halo, 0)
        gf_home(2)

    def own_slices():
        c_make(1, 7, 0)
        a_make(0)
        b_make(0)

    def to_line(t):
        plane_rings[t].third()
        line_rings[t].start()

    def unpack(value):
        v = value.astype(F32)
        return (
            jnp.concatenate([v[0:8], v[16:24]], axis=0).astype(BF16),
            jnp.concatenate([v[8:16], v[24:32]], axis=0).astype(BF16),
        )

    leaving = [
        pltpu.make_async_copy(src, dst, osem.at[i])
        for i, (src, dst) in enumerate((
            (att_out, att_hbm), (gq_out, gq_hbm), (gf_out, gf_hbm), (gk_out, gk_hbm),
            (gv_out, gv_hbm),
        ))
    ]

    def att_unpack():
        await_bytes(rag, gsem.at[0])
        for core in range(2):
            for pair in range(2):
                to = HALF * core + 256 * pair
                for out, at in ((att_out, 0), (gq_out, 256)):
                    for t in range(4):
                        part = rag[core, pair, 32 * t : 32 * t + 32, at : at + 256]
                        for fr, v in enumerate(unpack(part)):
                            out[fr, 16 * t : 16 * t + 16, to : to + 256] = v
        leaving[0].start()
        leaving[1].start()

    def gf_unpack():
        await_bytes(rgf, gsem.at[5])
        for t in range(4):
            for fr, v in enumerate(unpack(rgf[32 * t : 32 * t + 32, :])):
                gf_out[fr, 16 * t : 16 * t + 16, :] = v
        leaving[2].start()

    def z_sends():
        for r in range(1, NZ):
            sends.start(z_out.at[:, zi[r]], z_in.at[r - 1], endsem.at[0], zi[r] * PLANE + c, s)

    def c_last():
        for way, h, length, first in CHAINS:
            await_bytes(cb.at[first + length - 1], csem.at[first + length - 1])
        for h, (p, m) in enumerate(((3, 13), (10, 7))):
            own = c_view(0, h)

            def add(i, _):
                rc[2 * h + i] = (
                    own[i].astype(F32) + cb[p, i].astype(F32) + cb[m, i].astype(F32)
                ).astype(BF16)
                return 0

            lax.fori_loop(0, 2, add, 0)
        for r in range(1, PLANE):
            yy, xx = yi[r // 4], xi[r % 4]
            sends.start(rc.at[yy, xx], cc.at[r - 1], endsem.at[1], base + yy * 4 + xx, s)

    def halo_relay():
        for r in range(4):
            i = 4 * s + xi[r]
            block = rows_at(rows, 16 * i, 16)
            await_bytes(block, hsem.at[i])
            sends.start(block, block, got.at[2], base + c, 1 - s)

    def first_heads(tile):
        if tile == 1:
            await_bytes(qc.at[0], qsem.at[0])
        else:
            halo_relay()
            await_bytes(other(0), got.at[2])
            project(0)
        attend(0, tile)
        if tile == 0:
            g[:, :512] = acc[:, :512].astype(BF16)

    def second_heads(tile):
        if tile == 0:
            await_bytes(qc.at[1], qsem.at[1])
        attend(1, tile)
        if tile == 1:
            g[HALO:, 512:] = acc[HALO:, 512:].astype(BF16)

    def gf_halo():
        g[:HALO, 512:] = acc[:HALO, 512:].astype(BF16)
        gf_make(0, HALO)
        gf_cross(0)

    def gf_back():
        gf_add(0)
        sends.start(gx.at[pl.ds(0, 64)], gh, gsem.at[4], prv, s)

    steps = {
        "p01": lambda: first_heads(1), "p00": lambda: first_heads(0),
        "p10": lambda: second_heads(0), "p11": lambda: second_heads(1),
        "a01": lambda: ag_home(0, 1), "a00": lambda: ag_home(0, 0),
        "a11": lambda: ag_home(1, 1), "a10": lambda: ag_home(1, 0),
        "gfH": gf_halo, "gf0": gf_back,
        "T0": c_first, "B0": c_second, "F": ring_start, "gf": gf_own, "home1": gf_home1,
        "home2": gf_home2, "c26": lambda: c_make(2, 6), "c170": own_slices,
        "att": att_unpack, "gfout": gf_unpack, "Z": z_sends, "C": c_last,
    }
    for k in range(1, 4):
        steps["T%d" % k] = lambda k=k: c_step(CHAINS[:2], k)
        steps["B%d" % k] = lambda k=k: c_step(CHAINS[2:], k)
    for t in range(NT):
        steps["S%d" % t] = plane_rings[t].second
        steps["H%d" % t] = lambda t=t: to_line(t)
        steps["M%d" % t] = line_rings[t].finish
    for name in ORDER:
        steps[name]()

    def gathered(buf, own, count):
        return lax.fori_loop(0, count, lambda i, v: v + buf[i].astype(F32), own.astype(F32))

    await_bytes(z_in, endsem.at[0])
    for t in range(NT):
        out, at = (gk_out, 256 + 128 * t) if t < NA else (gv_out, 256 + 128 * (t - NA))
        out[:, at : at + 128] = gathered(z_in.at[:, t], z_out[t, z], NZ - 1)
    await_bytes(cc, endsem.at[1])
    last = gathered(cc, rc[y, x], PLANE - 1)
    gk_out[:, 0:256] = last[:, 0:256]
    gv_out[:, 0:256] = last[:, 256:512]
    leaving[3].start()
    leaving[4].start()
    sends.finish()
    for copy in leaving:
        copy.wait()


def leave_kernel(*refs):
    into, out = (
        [pltpu.make_async_copy(src[i], dst[i], sem.at[i]) for i in range(5)]
        for src, dst, sem in ((refs[0:5], refs[10:15], refs[15]), (refs[10:15], refs[5:10], refs[16]))
    )
    for copy in into:
        copy.start()
    for i in range(5):
        into[i].wait()
        out[i].start()
    for copy in out:
        copy.wait()


def shards(features, queries, cotangent, key_weight, value_weight):
    def vm(*shape, dtype=BF16):
        return pltpu.VMEM(shape, dtype)

    sem = pltpu.SemaphoreType.DMA
    t = NT
    scratch = [
        vm(2, 64, 1024), vm(2, 64, D), vm(2, 64, 1024), vm(16, HALF, dtype=F32),
        vm(16, HALF, dtype=F32),
        vm(2, 64, D), vm(2, 64, 2 * HALF), vm(2, 64, 2 * HALF),
        vm(D, HALF), vm(D, HALF), vm(128, D), vm(2, 2, 128, HALF),
        vm(ALL, D), vm(2, OWN, HALF), vm(8, 4, 4, 16, ALL),
        vm(ALL, HALF), vm(ALL, HALF), vm(ALL, 2 * HALF, dtype=F32), vm(ALL, 2 * HALF),
        vm(2, OWN, HALF), vm(ALL, D), vm(2, 2, 128, HALF), vm(128, D),
        vm(192, D), vm(64, D),
        vm(NA, 4, 8, 4, 16, 128), vm(NB, 4, 8, 4, 16, 128), vm(8, 4, 4, 16, CW),
        vm(t, 4, 4, 16, 128), vm(t, 4, 4, 16, 128), vm(t, 8, 4, 16, 128), vm(t, 8, 4, 16, 128),
        vm(t, 8, 4, 16, 128),
        vm(t, 3, 8, 16, 128),
        vm(t, 8, 16, 128), vm(NZ - 1, t, 16, 128),
        vm(14, 2, 4, 16, CW), vm(4, 4, 16, CW), vm(PLANE - 1, 16, CW),
        sem((200,)), sem((9,)), sem((3,)), sem((2,)), sem((16,)), sem((8,)), sem((6,)),
        sem((t, 6)), sem((t,)), sem((14,)), sem((2,)), sem((5,)),
    ]
    vmem = pl.BlockSpec(memory_space=pltpu.VMEM)
    hbm = pl.BlockSpec(memory_space=pl.ANY)
    results = pl.pallas_call(
        kernel,
        out_shape=(
            jax.ShapeDtypeStruct(queries.shape, BF16),
            jax.ShapeDtypeStruct(features.shape, BF16),
            jax.ShapeDtypeStruct(queries.shape, BF16),
            jax.ShapeDtypeStruct((16, HALF), F32),
            jax.ShapeDtypeStruct((16, HALF), F32),
        ),
        in_specs=[hbm] * 5,
        out_specs=[hbm] * 5,
        scratch_shapes=scratch,
        compiler_params=pltpu.CompilerParams(
            collective_id=0, has_side_effects=True, vmem_limit_bytes=61 * MIB
        ),
    )(features, queries, cotangent, key_weight, value_weight)
    return pl.pallas_call(
        leave_kernel,
        out_shape=tuple(jax.ShapeDtypeStruct(v.shape, v.dtype) for v in results),
        in_specs=[hbm] * 5,
        out_specs=[hbm] * 5,
        scratch_shapes=[pltpu.VMEM(v.shape, v.dtype) for v in results] + [sem((5,)), sem((5,))],
        compiler_params=pltpu.CompilerParams(vmem_limit_bytes=61 * MIB),
    )(*results)


def solution(mesh):
    rows = P("tm", "space", None)
    return jax.shard_map(
        shards,
        mesh=mesh,
        in_specs=(rows, rows, rows, P(None, "space"), P(None, "space")),
        out_specs=(rows, rows, rows, P("tm", "space"), P("tm", "space")),
        check_vma=False,
    )
```
